32 devices in a mesh: dp: 16 (over z, y, x), fsdp: 2 (over core).
Axes of the slice: x: 2, y: 2, z: 4, core: 2. Of those that a mesh axis runs over, the one named last changes fastest.
Arguments:
- inputs: bfloat16 [32768, 512], P(('dp', 'fsdp')), may hold values from -6 to 6
- cotangent: bfloat16 [32768, 512], P(('dp', 'fsdp')), may hold values from -6 to 6
- doc_ids: int32 [32, 1024], P(('dp', 'fsdp')), may hold values from 0 to 3, never falling along the last dimension, each value on 1 to 768 neighbouring positions
- slot_ids: int32 [32, 512, 4], P(('dp', 'fsdp')), may hold values from 0 to 511
- qkv_flat: bfloat16 [786432], P(('dp', 'fsdp')), may hold values from -0.375 to 0.375
- out_flat: bfloat16 [262144], P(('dp', 'fsdp')), may hold values from -1 to 1
- norm_gains: bfloat16 [1024], P(('dp', 'fsdp')), may hold values from 0.099609375 to 1.8984375
- gate_flat: bfloat16 [4096], P(('dp', 'fsdp')), may hold values from -0.25 to 0.25
- up_flat: bfloat16 [1048576], P(('dp', 'fsdp')), may hold values from -0.25 to 0.25
- down_flat: bfloat16 [1048576], P(('dp', 'fsdp')), may hold values from -0.125 to 0.125
Outputs:
- layer_out: bfloat16 [32768, 512], P(('dp', 'fsdp'))
- grad_input: bfloat16 [32768, 512], P(('dp', 'fsdp'))
- grad_qkv: float32 [786432], P(('dp', 'fsdp'))
- grad_out: float32 [262144], P(('dp', 'fsdp'))
- grad_gains: float32 [1024], P(('dp', 'fsdp'))
- grad_gate: float32 [4096], P(('dp', 'fsdp'))
- grad_up: float32 [1048576], P(('dp', 'fsdp'))
- grad_down: float32 [1048576], P(('dp', 'fsdp'))
The draws below stay inside these ranges and needn't reach their ends.
Inputs may be any that keep to these rules, and one draw needn't show every extreme that they name: `doc_ids`: along each sequence the document numbers start at 0 and never fall; each document covers 1 to 768 positions, and one of each sequence exactly that many. `slot_ids`: positions within the first segment of the same sequence.
All inputs are finite; a program needn't handle non-finite values.
Results may differ from the reference program's by a relative error of at most 0.012.
The reference program's roundings to bfloat16 on the way count: a program that leaves them out, or rounds other values in their place, can miss the bound.
Values may be sent and summed in bfloat16 or wider, within the bound.
No kernel may reach another device: no remote copies, remote signals or barrier semaphores. Data moves between devices by JAX's collectives and lax.ppermute only.
A program may use at most 192 MiB of HBM per device.

```python
import math
import jax
import jax.numpy as jnp
import numpy as np
from jax import lax

D = 512
H = 8
HD = 64
FF = 2048
SEG = 512
K = 4
DOCS = 4
SEQ = 1024
SEQS = 32
TOKENS = 32768


def plant(entries, stream_key, low, top_value):
    spot = [jax.random.randint(jax.random.fold_in(stream_key, axis), (), 0, length) for axis, length in enumerate(entries.shape)]
    main_axis = entries.shape.index(max(entries.shape))
    next_to = spot[:main_axis] + [(spot[main_axis] + 1) % entries.shape[main_axis]] + spot[main_axis + 1:]
    return entries.at[tuple(spot)].set(low).at[tuple(next_to)].set(top_value)


def levels(rng, extent, pieces, least, largest):
    level = 1.0
    for position, shards_of in pieces:
        steps = jax.random.uniform(jax.random.fold_in(jax.random.fold_in(rng, 6), position), (shards_of,), jnp.float32, least / len(pieces), largest / len(pieces))
        level = level * jnp.repeat(jnp.exp(steps), extent[position] // shards_of).reshape((-1,) + (1,) * (len(extent) - 1 - position))
    return level


def length_profile(amount, total, reach, slope):
    loads = [(1 << 20) // math.isqrt(rank ** slope) + 1 for rank in range(2, amount + 1)]
    rest, holding = total - reach - (amount - 1), [1] * (amount - 1)
    while rest > 0:
        free = [i for i in range(amount - 1) if holding[i] < reach]
        whole, budget = sum([loads[i] for i in free]), rest
        for i in free:
            more = min(reach - holding[i], max(1, budget * loads[i] // whole), rest)
            holding[i] = holding[i] + more
            rest = rest - more
    return np.array([reach] + holding)


def ragged(rng, number_of, total, most, skew):
    if number_of == 2:
        one = jax.random.randint(rng, (), max(1, total - most), min(most, total - 1) + 1)
        return jnp.stack([one, total - one])
    sizes = jnp.asarray(length_profile(number_of, total, most, skew), jnp.int32)
    pairs = (number_of - 1) // 2
    giver, sink = sizes[1:1 + 2 * pairs:2], sizes[2:2 + 2 * pairs:2]
    margin = jnp.minimum(giver - 1, most - sink)
    shifted = jax.random.randint(jax.random.fold_in(rng, 1), (pairs,), 0, 1 << 20) % (margin + 1)
    sizes = sizes.at[1:1 + 2 * pairs:2].set(giver - shifted).at[2:2 + 2 * pairs:2].set(sink + shifted)
    return sizes[jax.random.permutation(jax.random.fold_in(rng, 2), number_of)]


def scatter_about(own_key, extent, deviation, limit, shards=(), held_as=jnp.bfloat16):
    factor_of = levels(own_key, extent, shards, -0.22, 0.18) if shards else 1.0
    result = jax.random.normal(own_key, extent, jnp.float32) * deviation * factor_of
    return jnp.minimum(jnp.maximum(result, -limit), limit).astype(held_as)


def setup_inputs(seed: int = 0) -> dict:
    key_list = jax.random.split(jax.random.key(seed), 11)
    return {
        "inputs": scatter_about(key_list[0], (TOKENS, D), 1.0, 6.0, ((0, 32),)),
        "cotangent": scatter_about(key_list[1], (TOKENS, D), 1.0, 6.0, ((0, 32),)),
        "doc_ids": jax.vmap(lambda own: jnp.searchsorted(jnp.cumsum(ragged(own, DOCS, SEQ, 3 * SEG // 2, 2)), jnp.arange(SEQ), side="right"))(jax.random.split(key_list[2], SEQS)).reshape((SEQS, SEQ)).astype(jnp.int32),
        "slot_ids": plant(jax.random.randint(key_list[3], (SEQS, SEG, K), 0, SEG), jax.random.fold_in(key_list[3], 1), 0, SEG - 1).astype(jnp.int32),
        "qkv_flat": scatter_about(key_list[4], (3 * D * D,), (D // 2) ** -0.5, 0.375, ((0, 32),)),
        "out_flat": scatter_about(key_list[5], (D * D,), (D // 16) ** -0.5, 1.0, ((0, 32),)),
        "norm_gains": jnp.clip(1.0 + 0.18 * jax.random.normal(key_list[6], (2 * D,), jnp.float32), 0.099609375, 1.8984375).astype(jnp.bfloat16),
        "gate_flat": scatter_about(key_list[7], (D * H,), D ** -0.5, 0.25, ((0, 32),)),
        "up_flat": scatter_about(key_list[8], (D * FF,), D ** -0.5, 0.25, ((0, 32),)),
        "down_flat": scatter_about(key_list[9], (FF * D,), FF ** -0.5, 0.125, ((0, 32),)),
    }


@jax.custom_vjp
def low(v):
    return lax.optimization_barrier(v.astype(jnp.bfloat16)).astype(jnp.float32)

@jax.custom_vjp
def low_back(v):
    return v

def low_keep(v):
    return (low(v), None)

def low_pass(kept, grad):
    return (grad,)

def back_keep(v):
    return (v, None)

def back_low(kept, grad):
    return (low(grad),)
low.defvjp(low_keep, low_pass)
low_back.defvjp(back_keep, back_low)
precise = lax.Precision.HIGHEST

def rms_norm(values, gain_vec):
    factor = lax.rsqrt(lax.optimization_barrier(jnp.mean(values * values, axis=-1, keepdims=True)) + 1e-06)
    return values * factor * gain_vec

def block_attention(packed):
    queries, key_rows, value_rows, doc_block = packed
    seg_len = queries.shape[0]
    head_scale = 1.0 / math.sqrt(HD)
    query_h = queries.reshape(seg_len, H, HD)
    key_h = key_rows.reshape(seg_len, H, HD)
    value_h = value_rows.reshape(seg_len, H, HD)
    scores = low_back(jnp.einsum('ihd,jhd->hij', query_h, key_h, precision=precise) * head_scale)
    places = lax.broadcasted_iota(jnp.int32, (seg_len, seg_len), 0)
    sources = lax.broadcasted_iota(jnp.int32, (seg_len, seg_len), 1)
    allowed = (sources <= places) & (doc_block[:, None] == doc_block[None, :])
    scores = jnp.where(allowed[None], scores, -1e+30)
    attn_prob = low(jax.nn.softmax(scores, axis=2))
    local_h = jnp.einsum('hij,jhd->ihd', attn_prob, value_h, precision=precise)
    return low_back(local_h.reshape(seg_len, H * HD))

def pick_rows(table_rows, indices):
    return jax.vmap(lambda source_rows, picked: source_rows[picked])(table_rows, indices)

def layer(params, rows_in, doc_group, slot_group):
    qkv_flat, out_flat, norm_gains, gate_flat, up_flat, down_flat = params
    group_size = rows_in.shape[0]
    seq_len = rows_in.shape[1]
    seg_len = seq_len // 2
    row_count = group_size * seq_len
    block_count = group_size * 2
    head_scale = 1.0 / math.sqrt(HD)
    flat_in = rows_in.reshape(row_count, D)
    hid_one = low(rms_norm(flat_in, norm_gains[:D]))
    qkv_rows = low(low_back(jnp.dot(hid_one, qkv_flat.reshape(D, 3 * D), precision=precise)))
    query_rows = qkv_rows[:, :D]
    key_rows = qkv_rows[:, D:2 * D]
    value_rows = qkv_rows[:, 2 * D:]
    gate_prob = jax.nn.sigmoid(low_back(jnp.dot(hid_one, gate_flat.reshape(D, H), precision=precise)))
    packed = (query_rows.reshape(block_count, seg_len, D), key_rows.reshape(block_count, seg_len, D), value_rows.reshape(block_count, seg_len, D), doc_group.reshape(block_count, seg_len))
    local_out = lax.map(jax.checkpoint(block_attention), packed).reshape(row_count, D)
    query_two = query_rows.reshape(group_size, 2, seg_len, H, HD)[:, 1]
    key_first = key_rows.reshape(group_size, 2, seg_len, D)[:, 0]
    value_first = value_rows.reshape(group_size, 2, seg_len, D)[:, 0]
    doc_pairs = doc_group.reshape(group_size, 2, seg_len)
    key_ret = pick_rows(key_first, slot_group).reshape(group_size, seg_len, K, H, HD)
    value_ret = pick_rows(value_first, slot_group).reshape(group_size, seg_len, K, H, HD)
    valid = pick_rows(doc_pairs[:, 0], slot_group) == doc_pairs[:, 1][:, :, None]
    mem_score = jnp.einsum('nihd,nichd->nich', query_two, key_ret, precision=precise) * head_scale
    mem_score = jnp.where(valid[:, :, :, None], mem_score, -1e+30)
    null_col = jnp.zeros((group_size, seg_len, 1, H), jnp.float32)
    mem_prob = jax.nn.softmax(jnp.concatenate([null_col, mem_score], axis=2), axis=2)[:, :, 1:]
    mem_two = jnp.einsum('nich,nichd->nihd', mem_prob, value_ret, precision=precise).reshape(group_size, seg_len, D)
    mem_out = jnp.stack([jnp.zeros_like(mem_two), mem_two], axis=1).reshape(row_count, D)
    gate_wide = jnp.repeat(gate_prob, HD, axis=1)
    mixed = low(low_back(gate_wide * local_out + (1.0 - gate_wide) * mem_out))
    resid = flat_in + low_back(jnp.dot(mixed, out_flat.reshape(D, D), precision=precise))
    hid_two = low(rms_norm(resid, norm_gains[D:]))
    upper = low_back(jnp.dot(hid_two, up_flat.reshape(D, FF), precision=precise))
    act_rows = low(jax.nn.gelu(upper))
    final = resid + low_back(jnp.dot(act_rows, down_flat.reshape(FF, D), precision=precise))
    return final.reshape(group_size, seq_len, D)

def reference(inputs, cotangent, doc_ids, slot_ids, qkv_flat, out_flat, norm_gains, gate_flat, up_flat, down_flat):
    params = (qkv_flat.astype(jnp.float32), out_flat.astype(jnp.float32), norm_gains.astype(jnp.float32), gate_flat.astype(jnp.float32), up_flat.astype(jnp.float32), down_flat.astype(jnp.float32))
    seq_count = doc_ids.shape[0]
    seq_len = doc_ids.shape[1]
    group_size = 4 if seq_count % 4 == 0 else 1
    step_count = seq_count // group_size
    rows_all = inputs.astype(jnp.float32).reshape(step_count, group_size, seq_len, D)
    cot_all = cotangent.astype(jnp.float32).reshape(step_count, group_size, seq_len, D)
    docs_all = doc_ids.reshape(step_count, group_size, seq_len)
    slots_all = slot_ids.reshape(step_count, group_size, seq_len // 2, K)

    def one_step(totals, packed):
        rows_in, cot_in, doc_group, slot_group = packed

        def forward(weights_in, values_in):
            return layer(weights_in, values_in, doc_group, slot_group)
        final, pullback = jax.vjp(forward, params, rows_in)
        grad_params, grad_rows = pullback(cot_in)
        totals = tuple((first + second for first, second in zip(totals, grad_params)))
        return (totals, (final.astype(jnp.bfloat16), grad_rows.astype(jnp.bfloat16)))
    starting = tuple((jnp.zeros_like(weight_arr) for weight_arr in params))
    totals, outputs = lax.scan(one_step, starting, (rows_all, cot_all, docs_all, slots_all))
    layer_out = outputs[0].reshape(seq_count * seq_len, D)
    grad_input = outputs[1].reshape(seq_count * seq_len, D)
    return (layer_out, grad_input, totals[0], totals[1], totals[2], totals[3], totals[4], totals[5])
```

```python
import jax
import jax.numpy as jnp
from jax import lax
from jax.experimental import pallas as pl
from jax.experimental.pallas import tpu as pltpu
from jax.sharding import PartitionSpec as P

D = 512
H = 8
HD = 64
K = 4
FF = 2048
SEQ = 1024
SEG = 512
PIECES = 32
ROWS = D // PIECES
EXT = 3 * D + 128
GCOL = 8
GLEN = 2 * D // PIECES
NEG = -1e30
BF = jnp.bfloat16
F32 = jnp.float32
AXES = ("dp", "fsdp")
NT = (((1,), (1,)), ((), ()))
TN = (((0,), (0,)), ((), ()))
ANY = pl.BlockSpec(memory_space=pl.ANY)
VLIMIT = 60 * 1024 * 1024


def mm(a, b):
    return jnp.dot(a, b, preferred_element_type=F32)


def mm_nt(a, b):
    return lax.dot_general(a, b, NT, preferred_element_type=F32)


def mm_tn(a, b):
    return lax.dot_general(a, b, TN, preferred_element_type=F32)


def perm_z(v, shift):
    return lax.ppermute(v, "dp", [(i, (i + 4 * shift) % 16) for i in range(16)])


def perm_bit(v, bit):
    return lax.ppermute(v, "dp", [(i, i ^ bit) for i in range(16)])


def perm_core(v):
    return lax.ppermute(v, "fsdp", [(0, 1), (1, 0)])


def gather_z(shard):
    return jnp.stack([shard] + [perm_z(shard, -k) for k in (1, 2, 3)])


def gather_rest(stacked, first, second):
    wider = jnp.concatenate([stacked, perm_bit(stacked, first)])
    wider = jnp.concatenate([wider, perm_bit(wider, second)])
    return (wider, perm_core(wider))


def reduce_core(keep, send):
    return keep.astype(F32) + perm_core(send).astype(F32)


def reduce_bit(total, bit):
    half = total.shape[0] // 2
    return total[:half] + perm_bit(total[half:].astype(BF), bit).astype(F32)


def reduce_z(total):
    out = total[0]
    for k in (1, 2, 3):
        out = out + perm_z(total[k].astype(BF), k).astype(F32)
    return out


def piece_owner(piece, x_first):
    place = lax.axis_index("dp")
    z, y, x = place >> 2, (place >> 1) & 1, place & 1
    kz, low, high, kc = piece & 3, (piece >> 2) & 1, (piece >> 3) & 1, piece >> 4
    kx, ky = (low, high) if x_first else (high, low)
    chip = ((((z + kz) & 3) * 2 + (y ^ ky)) * 2) + (x ^ kx)
    return chip * 2 + (lax.axis_index("fsdp") ^ kc)


def owner_fn(relative, x_first):
    if relative:
        return lambda piece: piece_owner(piece, x_first)
    return lambda piece: piece


def bias_kernel(doc_row, doc_col, slots, bias):
    sources = lax.broadcasted_iota(jnp.int32, (SEG, SEG), 0)
    places = lax.broadcasted_iota(jnp.int32, (SEG, SEG), 1)
    for seg in range(2):
        part = slice(seg * SEG, (seg + 1) * SEG)
        same = doc_col[part, :] == doc_row[:, part]
        bias[seg] = jnp.where((sources <= places) & same, 0.0, NEG)
    count = jnp.zeros((SEG, SEG), F32)
    for c in range(K):
        count = count + jnp.where(sources == slots[c : c + 1, :], 1.0, 0.0)
    kept = (doc_col[0:SEG, :] == doc_row[:, SEG : 2 * SEG]) & (count > 0.0)
    bias[2] = jnp.where(kept, jnp.log(jnp.maximum(count, 1.0)), NEG)


def rows_from_ext(ext):
    pick = lax.broadcasted_iota(jnp.int32, (PIECES, D), 1) == ROWS * lax.broadcasted_iota(
        jnp.int32, (PIECES, D), 0
    )
    gains = mm(pick.astype(BF), ext).astype(BF)
    source = lax.broadcasted_iota(jnp.int32, (128, D), 0) - GCOL
    column = lax.broadcasted_iota(jnp.int32, (128, D), 1)
    spread = mm(gains, (source == (column & (GLEN - 1))).astype(BF))
    piece = lax.broadcasted_iota(jnp.int32, (PIECES, D), 0)
    block = lax.broadcasted_iota(jnp.int32, (PIECES, D), 1) // GLEN
    one = jnp.sum(jnp.where(block == piece, spread, 0.0), axis=0, keepdims=True)
    two = jnp.sum(jnp.where(block + D // GLEN == piece, spread, 0.0), axis=0, keepdims=True)
    return one, two


def ext_from_rows(one, two):
    piece = lax.broadcasted_iota(jnp.int32, (PIECES, D), 0)
    block = lax.broadcasted_iota(jnp.int32, (PIECES, D), 1) // GLEN
    laid = jnp.where(block == piece, one, 0.0) + jnp.where(block + D // GLEN == piece, two, 0.0)
    column = lax.broadcasted_iota(jnp.int32, (D, 128), 0)
    target = lax.broadcasted_iota(jnp.int32, (D, 128), 1) - GCOL
    packed = mm(laid.astype(BF), (target == (column & (GLEN - 1))).astype(BF)).astype(BF)
    pick = lax.broadcasted_iota(jnp.int32, (D, PIECES), 0) == ROWS * lax.broadcasted_iota(
        jnp.int32, (D, PIECES), 1
    )
    return mm(pick.astype(BF), packed)


def start_pieces(parts, owner, make):
    base = 0
    for part in parts:
        for i in range(part.shape[0]):
            make(part.at[i], owner(base + i)).start()
        base += part.shape[0]


def head_half(rows, upper_half):
    blank = jnp.zeros_like(rows)
    return jnp.concatenate([blank, rows] if upper_half else [rows, blank], axis=0)


def attention_forward_kernel(owner, count_a, count_b, *refs):
    x, bias = refs[:2]
    parts_a = refs[2 : 2 + count_a]
    parts_b = refs[2 + count_a : 2 + count_a + count_b]
    outs = refs[2 + count_a + count_b :]
    qkvt_o, vtok_o, hidt_o, w_o, gatet, gains, probs, local_t, mem_t, inv_sums, mixed_t, mixed = (
        outs[:12]
    )
    w_vm, ktok, vtok, qkvt, hidt, in_sem, out_sem = outs[12:]
    pair = pl.program_id(0)
    half = w_vm.shape[1] - parts_b[0].shape[2]

    @pl.when(pair == 0)
    def _():
        start_pieces(
            parts_a,
            owner[0],
            lambda src, d: pltpu.make_async_copy(
                src,
                w_vm.at[pl.ds(pl.multiple_of(d * ROWS, ROWS), ROWS), pl.ds(0, half)],
                in_sem,
            ),
        )
        start_pieces(
            parts_b,
            owner[1],
            lambda src, d: pltpu.make_async_copy(
                src,
                w_vm.at[pl.ds(pl.multiple_of(d * ROWS, ROWS), ROWS), pl.ds(half, EXT - half)],
                in_sem,
            ),
        )
        pltpu.make_async_copy(w_o, w_vm, in_sem).wait()
        g_one, g_two = rows_from_ext(w_vm[:, 3 * D :])
        gains[...] = jnp.concatenate([g_one, g_two], axis=0)

        @pl.loop(0, 4)
        def _(block):
            rows = pl.ds(pl.multiple_of(block * 256, 256), 256)
            xf = x[rows, :].astype(F32)
            factor = lax.rsqrt(jnp.mean(xf * xf, axis=1, keepdims=True) + 1e-06)
            hid = (xf * factor * g_one).astype(BF)
            out = mm(hid, w_vm[...])
            ktok[rows, :] = out[:, D : 2 * D].astype(BF)
            vtok[rows, :] = out[:, 2 * D : 3 * D].astype(BF)
            qkvt[0:D, rows] = (out[:, :D].astype(BF) * 0.125).T
            qkvt[D : 2 * D, rows] = out[:, D : 2 * D].astype(BF).T
            qkvt[2 * D : 3 * D, rows] = out[:, 2 * D : 3 * D].astype(BF).T
            gatet[:, rows] = jax.nn.sigmoid(out[:, 3 * D :]).T[0:H, :]
            hidt[:, rows] = hid.T

        pltpu.make_async_copy(qkvt, qkvt_o, out_sem.at[0]).start()
        pltpu.make_async_copy(vtok, vtok_o, out_sem.at[1]).start()
        pltpu.make_async_copy(hidt, hidt_o, out_sem.at[2]).start()
        pltpu.make_async_copy(w_vm, w_o, out_sem.at[3]).start()

    lanes = pl.ds(pl.multiple_of(pair * 128, 128), 128)

    def head_rows(third, hh, columns):
        start = pl.multiple_of(third * D + pair * 128 + hh * HD, HD)
        return qkvt[pl.ds(start, HD), columns]

    for hh in range(2):
        rows = slice(hh * HD, (hh + 1) * HD)
        gate = gatet[pl.ds(2 * pair + hh, 1), :]
        base = 0
        for seg in range(3):
            for ib in range(2):
                key_first = SEG if seg == 1 else 0
                key_count = SEG if seg == 2 else 256 * (ib + 1)
                column = (0 if seg == 0 else SEG) + 256 * ib
                query = head_half(head_rows(0, hh, slice(column, column + 256)), hh)
                keys = ktok[key_first : key_first + key_count, lanes]
                score = mm(keys, query) + bias[seg, 0:key_count, 256 * ib : 256 * ib + 256]
                peak = jnp.max(score, axis=0, keepdims=True)
                if seg == 2:
                    peak = jnp.maximum(peak, 0.0)
                expo = jnp.exp(score - peak)
                total = jnp.sum(expo, axis=0, keepdims=True)
                if seg == 2:
                    total = total + jnp.exp(-peak)
                expo_b = expo.astype(BF)
                probs[0, hh, base : base + key_count, :] = expo_b
                base += key_count
                inverse = 1.0 / total
                value = head_rows(2, hh, slice(key_first, key_first + key_count))
                found = mm(value, expo_b) * inverse
                if seg < 2:
                    local_t[rows, column : column + 256] = found
                    inv_sums[0, hh : hh + 1, column : column + 256] = inverse
                    if seg == 0:
                        mixed_t[rows, column : column + 256] = (
                            gate[:, column : column + 256] * found
                        ).astype(BF)
                else:
                    mem_t[rows, 256 * ib : 256 * ib + 256] = found
                    inv_sums[0, 2 + hh : 3 + hh, column - SEG : column - SEG + 256] = inverse
                    here = gate[:, column : column + 256]
                    mixed_t[rows, column : column + 256] = (
                        here * local_t[rows, column : column + 256] + (1.0 - here) * found
                    ).astype(BF)
    inv_sums[0, 2:4, SEG:] = jnp.zeros((2, SEG), F32)
    mixed[...] = mixed_t[...].T

    @pl.when(pair == 3)
    def _():
        pltpu.make_async_copy(qkvt, qkvt_o, out_sem.at[0]).wait()
        pltpu.make_async_copy(vtok, vtok_o, out_sem.at[1]).wait()
        pltpu.make_async_copy(hidt, hidt_o, out_sem.at[2]).wait()
        pltpu.make_async_copy(w_vm, w_o, out_sem.at[3]).wait()


PROB_ROWS = 2 * 768 + 1024


def attention_forward(x, bias, parts_a, parts_b, owner):
    const2 = lambda p: (0, 0)

    def body(*refs):
        attention_forward_kernel(owner, len(parts_a), len(parts_b), *refs)

    return pl.pallas_call(
        body,
        grid=(4,),
        in_specs=[
            pl.BlockSpec((SEQ, D), const2),
            pl.BlockSpec((3, SEG, SEG), lambda p: (0, 0, 0)),
        ]
        + [ANY] * (len(parts_a) + len(parts_b)),
        out_specs=[
            ANY,
            ANY,
            ANY,
            ANY,
            pl.BlockSpec((H, SEQ), const2),
            pl.BlockSpec((2, D), const2),
            pl.BlockSpec((1, 2, PROB_ROWS, 256), lambda p: (p, 0, 0, 0)),
            pl.BlockSpec((128, SEQ), lambda p: (p, 0)),
            pl.BlockSpec((128, SEG), lambda p: (p, 0)),
            pl.BlockSpec((1, 4, SEQ), lambda p: (p, 0, 0)),
            pl.BlockSpec((128, SEQ), lambda p: (p, 0)),
            pl.BlockSpec((SEQ, 128), lambda p: (0, p)),
        ],
        out_shape=[
            jax.ShapeDtypeStruct((3 * D, SEQ), BF),
            jax.ShapeDtypeStruct((SEQ, D), BF),
            jax.ShapeDtypeStruct((D, SEQ), BF),
            jax.ShapeDtypeStruct((D, EXT), BF),
            jax.ShapeDtypeStruct((H, SEQ), F32),
            jax.ShapeDtypeStruct((2, D), F32),
            jax.ShapeDtypeStruct((4, 2, PROB_ROWS, 256), BF),
            jax.ShapeDtypeStruct((D, SEQ), F32),
            jax.ShapeDtypeStruct((D, SEG), F32),
            jax.ShapeDtypeStruct((4, 4, SEQ), F32),
            jax.ShapeDtypeStruct((D, SEQ), BF),
            jax.ShapeDtypeStruct((SEQ, D), BF),
        ],
        scratch_shapes=[
            pltpu.VMEM((D, EXT), BF),
            pltpu.VMEM((SEQ, D), BF),
            pltpu.VMEM((SEQ, D), BF),
            pltpu.VMEM((3 * D, SEQ), BF),
            pltpu.VMEM((D, SEQ), BF),
            pltpu.SemaphoreType.DMA,
            pltpu.SemaphoreType.DMA((4,)),
        ],
        compiler_params=pltpu.CompilerParams(vmem_limit_bytes=VLIMIT),
        cost_estimate=pl.CostEstimate(
            flops=12_000_000_000, bytes_accessed=30_000_000, transcendentals=6_000_000
        ),
        name="attention_forward",
    )(x, bias, *parts_a, *parts_b)


def ffn_kernel(owner_u, owner_d, count_u, count_d, split, *refs):
    x, cot, mixed, mixed_t, gains = refs[:5]
    parts_u = refs[5 : 5 + count_u]
    parts_d = refs[5 + count_u : 5 + count_u + count_d]
    outs = refs[5 + count_u + count_d :]
    layer_out, d_resid_o, dmix_t, dgain = outs[:4]
    count_o = 2 if split else 1
    grads_u = outs[4 : 4 + count_o]
    grads_d = outs[4 + count_o : 4 + 2 * count_o]
    rest = outs[4 + 2 * count_o :]
    w_out, w_up, w_dn, resid, hid, hidt, oacc, dacc, g_out, g_up, g_dn, in_sem, out_sem = rest
    step = pl.program_id(0)
    per = PIECES // count_o

    @pl.when(step == 0)
    def _():
        def load_u(first):
            def make(src, d):
                rows = pl.ds(pl.multiple_of(d * ROWS, ROWS), ROWS)
                if first:
                    return pltpu.make_async_copy(src.at[0], w_out.at[rows, :], in_sem.at[0])
                return pltpu.make_async_copy(
                    src.at[pl.ds(1, 4)], w_up.at[:, rows, :], in_sem.at[1]
                )

            return make

        start_pieces(parts_u, owner_u, load_u(True))
        start_pieces(parts_u, owner_u, load_u(False))
        start_pieces(
            parts_d,
            owner_d,
            lambda src, d: pltpu.make_async_copy(
                src, w_dn.at[pl.ds(pl.multiple_of(d * 64, 64), 64), :], in_sem.at[2]
            ),
        )
        pltpu.make_async_copy(g_out, w_out, in_sem.at[0]).wait()

        @pl.loop(0, 4)
        def _(block):
            rows = pl.ds(pl.multiple_of(block * 256, 256), 256)
            value = x[rows, :].astype(F32) + mm(mixed[rows, :], w_out[...])
            factor = lax.rsqrt(jnp.mean(value * value, axis=1, keepdims=True) + 1e-06)
            normed = (value * factor * gains[1:2, :]).astype(BF)
            resid[rows, :] = value
            hid[rows, :] = normed
            hidt[:, rows] = normed.T

        oacc[...] = jnp.zeros_like(oacc)
        dacc[...] = jnp.zeros_like(dacc)
        pltpu.make_async_copy(g_up, w_up, in_sem.at[1]).wait()
        pltpu.make_async_copy(g_dn, w_dn, in_sem.at[2]).wait()

    quarter = step // 2
    lanes = pl.ds(pl.multiple_of((step % 2) * 256, 256), 256)
    ff_rows = pl.ds(pl.multiple_of(step * 256, 256), 256)
    wu = w_up[quarter, :, lanes]
    wd = w_dn[ff_rows, :]
    upper = mm(hid[...], wu)
    c0 = 0.7978845608028654
    c1 = 0.044715
    square = upper * upper
    tanh = jnp.tanh(c0 * upper * (1.0 + c1 * square))
    half_t = 0.5 * tanh + 0.5
    act = (upper * half_t).astype(BF)
    slope = half_t + 0.5 * upper * (1.0 - tanh * tanh) * (c0 * (1.0 + 3.0 * c1 * square))
    d_act = mm_nt(cot[...], wd)
    d_up = (d_act * slope).astype(BF)
    oacc[...] += mm(act, wd)
    g_dn[ff_rows, :] = mm_tn(act, cot[...]).astype(BF)
    g_up[quarter, :, lanes] = mm(hidt[...], d_up).astype(BF)
    dacc[...] += mm_nt(d_up, wu)

    @pl.when(step == 7)
    def _():
        for piece in range(PIECES):
            d = owner_d(piece)
            pltpu.make_async_copy(
                g_dn.at[pl.ds(pl.multiple_of(d * 64, 64), 64), :],
                grads_d[piece // per].at[piece % per],
                out_sem.at[0],
            ).start()
            d = owner_u(piece)
            pltpu.make_async_copy(
                g_up.at[:, pl.ds(pl.multiple_of(d * ROWS, ROWS), ROWS), :],
                grads_u[piece // per].at[piece % per, pl.ds(1, 4)],
                out_sem.at[1],
            ).start()
        g_two = gains[1:2, :]
        dgain[...] = jnp.zeros_like(dgain)

        @pl.loop(0, 4)
        def _(block):
            rows = pl.ds(pl.multiple_of(block * 256, 256), 256)
            value = resid[rows, :]
            factor = lax.rsqrt(jnp.mean(value * value, axis=1, keepdims=True) + 1e-06)
            layer_out[rows, :] = (value + oacc[rows, :]).astype(BF)
            d_hid = dacc[rows, :]
            dgain[...] += jnp.sum(d_hid * value * factor, axis=0, keepdims=True)
            scaled = d_hid * g_two
            inner = jnp.mean(scaled * value, axis=1, keepdims=True)
            d_resid = cot[rows, :].astype(F32) + (
                factor * scaled - value * (factor * factor * factor * inner)
            )
            d_resid_o[rows, :] = d_resid
            d_resid_b = d_resid.astype(BF)
            hid[rows, :] = d_resid_b
            dmix_t[:, rows] = mm_nt(w_out[...], d_resid_b).astype(BF)

        g_out[...] = mm(mixed_t[...], hid[...]).astype(BF)
        for piece in range(PIECES):
            d = owner_u(piece)
            pltpu.make_async_copy(
                g_out.at[pl.ds(pl.multiple_of(d * ROWS, ROWS), ROWS), :],
                grads_u[piece // per].at[piece % per, 0],
                out_sem.at[2],
            ).start()
        pltpu.make_async_copy(g_dn, w_dn, out_sem.at[0]).wait()
        pltpu.make_async_copy(g_up, w_up, out_sem.at[1]).wait()
        pltpu.make_async_copy(g_out, w_out, out_sem.at[2]).wait()


def ffn(x, cot, mixed, mixed_t, gains, parts_u, parts_d, owner_u, owner_d, split):
    count_o = 2 if split else 1
    whole = pl.BlockSpec(memory_space=pltpu.VMEM)

    def body(*refs):
        ffn_kernel(owner_u, owner_d, len(parts_u), len(parts_d), split, *refs)

    const2 = lambda p: (0, 0)
    return pl.pallas_call(
        body,
        grid=(8,),
        in_specs=[
            pl.BlockSpec((SEQ, D), const2),
            pl.BlockSpec((SEQ, D), const2),
            pl.BlockSpec((SEQ, D), const2),
            pl.BlockSpec((D, SEQ), const2),
            pl.BlockSpec((2, D), const2),
        ]
        + [ANY] * (len(parts_u) + len(parts_d)),
        out_specs=[
            pl.BlockSpec((SEQ, D), const2),
            pl.BlockSpec((SEQ, D), const2),
            pl.BlockSpec((D, SEQ), const2),
            pl.BlockSpec((1, D), const2),
        ]
        + [ANY] * (2 * count_o),
        out_shape=[
            jax.ShapeDtypeStruct((SEQ, D), BF),
            jax.ShapeDtypeStruct((SEQ, D), F32),
            jax.ShapeDtypeStruct((D, SEQ), BF),
            jax.ShapeDtypeStruct((1, D), F32),
        ]
        + [jax.ShapeDtypeStruct((PIECES // count_o, 5, ROWS, D), BF)] * count_o
        + [jax.ShapeDtypeStruct((PIECES // count_o, 64, D), BF)] * count_o,
        scratch_shapes=[
            pltpu.VMEM((D, D), BF),
            pltpu.VMEM((4, D, D), BF),
            pltpu.VMEM((FF, D), BF),
            pltpu.VMEM((SEQ, D), F32),
            pltpu.VMEM((SEQ, D), BF),
            pltpu.VMEM((D, SEQ), BF),
            pltpu.VMEM((SEQ, D), F32),
            pltpu.VMEM((SEQ, D), F32),
            pltpu.VMEM((D, D), BF),
            pltpu.VMEM((4, D, D), BF),
            pltpu.VMEM((FF, D), BF),
            pltpu.SemaphoreType.DMA((3,)),
            pltpu.SemaphoreType.DMA((3,)),
        ],
        compiler_params=pltpu.CompilerParams(vmem_limit_bytes=VLIMIT),
        cost_estimate=pl.CostEstimate(
            flops=15_000_000_000, bytes_accessed=20_000_000, transcendentals=2_000_000
        ),
        name="feed_forward",
    )(x, cot, mixed, mixed_t, gains, *parts_u, *parts_d)


def attention_backward_kernel(owner, split, *refs):
    (x, d_resid, dgain_two, gains, gatet, w, hidt, probs, local_t, mem_t, inv_sums, dmix_t) = refs[
        :12
    ]
    qt, kt, vt, vtok = refs[12:16]
    count_o = 2 if split else 1
    grad_in = refs[16]
    grads = refs[17 : 17 + count_o]
    dqkvt, g_ext, out_sem = refs[17 + count_o :]
    pair = pl.program_id(0)
    per = PIECES // count_o

    @pl.when(pair == 0)
    def _():
        dqkvt[3 * D :, :] = jnp.zeros((128, SEQ), BF)

    for hh in range(2):
        rows = slice(hh * HD, (hh + 1) * HD)
        head = 2 * pair + hh
        gate = gatet[pl.ds(head, 1), :]
        d_mix = dmix_t[rows, :].astype(F32)
        local = local_t[rows, :]
        mem = mem_t[rows, :]
        inv_local = inv_sums[0, hh : hh + 1, :]
        inv_mem = inv_sums[0, 2 + hh : 3 + hh, 0:SEG]
        d_local = (d_mix * (gate * inv_local)).astype(BF)
        d_mem = (d_mix[:, SEG:] * ((1.0 - gate[:, SEG:]) * inv_mem)).astype(BF)
        dot_local = jnp.sum(d_local.astype(F32) * local, axis=0, keepdims=True)
        dot_mem = jnp.sum(d_mem.astype(F32) * mem, axis=0, keepdims=True)
        plain_local = jnp.sum(d_mix * local, axis=0, keepdims=True)
        plain_mem = jnp.sum(d_mix[:, SEG:] * mem, axis=0, keepdims=True)
        d_gate = gate * (1.0 - gate) * (
            plain_local - jnp.concatenate([jnp.zeros((1, SEG), F32), plain_mem], axis=1)
        )
        slot = lax.broadcasted_iota(jnp.int32, (16, SEQ), 0) == head
        dqkvt[3 * D : 3 * D + 16, :] = jnp.where(slot, d_gate.astype(BF), dqkvt[3 * D : 3 * D + 16, :])
        d_key = [jnp.zeros((HD, SEG), F32), jnp.zeros((HD, SEG), F32)]
        d_value = [jnp.zeros((HD, SEG), F32), jnp.zeros((HD, SEG), F32)]
        d_query = [None] * 4
        base = 0
        for seg in range(3):
            for ib in range(2):
                side = 1 if seg == 1 else 0
                key_first = side * SEG
                key_count = SEG if seg == 2 else 256 * (ib + 1)
                column = (0 if seg == 0 else SEG) + 256 * ib
                place = column // 256
                expo = probs[0, hh, base : base + key_count, :]
                base += key_count
                if seg == 2:
                    up = d_mem[:, 256 * ib : 256 * ib + 256]
                    dot = dot_mem[:, 256 * ib : 256 * ib + 256]
                else:
                    up = d_local[:, column : column + 256]
                    dot = dot_local[:, column : column + 256]
                d_prob = mm(vtok[key_first : key_first + key_count, :], head_half(up, hh))
                d_score = (expo.astype(F32) * (d_prob - dot)).astype(BF)
                term = mm(kt[rows, key_first : key_first + key_count], d_score)
                d_query[place] = term if d_query[place] is None else d_query[place] + term
                key_term = mm_nt(qt[rows, column : column + 256], d_score)
                value_term = mm_nt(up, expo)
                if key_count < SEG:
                    blank = jnp.zeros((HD, SEG - key_count), F32)
                    key_term = jnp.concatenate([key_term, blank], axis=1)
                    value_term = jnp.concatenate([value_term, blank], axis=1)
                d_key[side] = d_key[side] + key_term
                d_value[side] = d_value[side] + value_term
        for place in range(4):
            start = pl.multiple_of(pair * 128 + hh * HD, HD)
            dqkvt[pl.ds(start, HD), 256 * place : 256 * place + 256] = (
                d_query[place] * 0.125
            ).astype(BF)
        for side in range(2):
            columns = slice(side * SEG, (side + 1) * SEG)
            start = pl.multiple_of(D + pair * 128 + hh * HD, HD)
            dqkvt[pl.ds(start, HD), columns] = d_key[side].astype(BF)
            start = pl.multiple_of(2 * D + pair * 128 + hh * HD, HD)
            dqkvt[pl.ds(start, HD), columns] = d_value[side].astype(BF)

    @pl.when(pair == 3)
    def _():
        g_one = gains[0:1, :]
        total = jnp.zeros((1, D), F32)

        @pl.loop(0, 4)
        def _(block):
            lanes = pl.ds(pl.multiple_of(block * 384, 128), 384)
            g_ext[:, lanes] = mm_nt(hidt[...], dqkvt[lanes, :]).astype(BF)

        def row_block(block, total):
            rows = pl.ds(pl.multiple_of(block * 256, 256), 256)
            d_hid = mm(w[...], dqkvt[:, rows]).T
            xf = x[rows, :].astype(F32)
            factor = lax.rsqrt(jnp.mean(xf * xf, axis=1, keepdims=True) + 1e-06)
            total = total + jnp.sum(d_hid * xf * factor, axis=0, keepdims=True)
            scaled = d_hid * g_one
            inner = jnp.mean(scaled * xf, axis=1, keepdims=True)
            grad_in[rows, :] = (
                d_resid[rows, :] + factor * scaled - xf * (factor * factor * factor * inner)
            ).astype(BF)
            return total

        total = lax.fori_loop(0, 4, row_block, total)
        last = mm_nt(hidt[...], dqkvt[3 * D :, :]) + ext_from_rows(total, dgain_two[...])
        g_ext[:, 3 * D :] = last.astype(BF)
        for piece in range(PIECES):
            d = owner(piece)
            pltpu.make_async_copy(
                g_ext.at[pl.ds(pl.multiple_of(d * ROWS, ROWS), ROWS), :],
                grads[piece // per].at[piece % per],
                out_sem,
            ).start()
        pltpu.make_async_copy(g_ext, w, out_sem).wait()


def attention_backward(
    x, d_resid, dgain, gains, gatet, w, hidt, probs, local_t, mem_t, inv_sums, dmix_t, qkvt, vtok, owner, split
):
    count_o = 2 if split else 1
    const2 = lambda p: (0, 0)

    def body(*refs):
        attention_backward_kernel(owner, split, *refs)

    return pl.pallas_call(
        body,
        grid=(4,),
        in_specs=[
            pl.BlockSpec((SEQ, D), const2),
            pl.BlockSpec((SEQ, D), const2),
            pl.BlockSpec((1, D), const2),
            pl.BlockSpec((2, D), const2),
            pl.BlockSpec((H, SEQ), const2),
            pl.BlockSpec((D, EXT), const2),
            pl.BlockSpec((D, SEQ), const2),
            pl.BlockSpec((1, 2, PROB_ROWS, 256), lambda p: (p, 0, 0, 0)),
            pl.BlockSpec((128, SEQ), lambda p: (p, 0)),
            pl.BlockSpec((128, SEG), lambda p: (p, 0)),
            pl.BlockSpec((1, 4, SEQ), lambda p: (p, 0, 0)),
            pl.BlockSpec((128, SEQ), lambda p: (p, 0)),
            pl.BlockSpec((128, SEQ), lambda p: (p, 0)),
            pl.BlockSpec((128, SEQ), lambda p: (4 + p, 0)),
            pl.BlockSpec((128, SEQ), lambda p: (8 + p, 0)),
            pl.BlockSpec((SEQ, 128), lambda p: (0, p)),
        ],
        out_specs=[pl.BlockSpec((SEQ, D), const2)] + [ANY] * count_o,
        out_shape=[jax.ShapeDtypeStruct((SEQ, D), BF)]
        + [jax.ShapeDtypeStruct((PIECES // count_o, ROWS, EXT), BF)] * count_o,
        scratch_shapes=[
            pltpu.VMEM((EXT, SEQ), BF),
            pltpu.VMEM((D, EXT), BF),
            pltpu.SemaphoreType.DMA,
        ],
        compiler_params=pltpu.CompilerParams(vmem_limit_bytes=VLIMIT),
        cost_estimate=pl.CostEstimate(
            flops=15_000_000_000, bytes_accessed=30_000_000, transcendentals=0
        ),
        name="attention_backward",
    )(x, d_resid, dgain, gains, gatet, w, hidt, probs, local_t, mem_t, inv_sums, dmix_t, qkvt, qkvt, qkvt, vtok)


def ext_rows(qkv, gate, gains):
    count = qkv.shape[0]
    blank = jnp.zeros((count, 128 - GCOL - gains.shape[1]), BF)
    return jnp.concatenate([qkv, gate, gains, blank], axis=1)


def local(
    n, inputs, cotangent, doc_ids, slot_ids, qkv_flat, out_flat, norm_gains, gate_flat, up_flat, down_flat
):
    split = n == PIECES
    doc_row = doc_ids.reshape(1, SEQ)
    doc_col = doc_ids.reshape(SEQ, 1)
    slots = slot_ids.reshape(SEG, K).T
    half = 7 * 128
    if split:
        gains_rows = jnp.broadcast_to(norm_gains.reshape(1, GLEN), (ROWS, GLEN))
        shard_a = ext_rows(qkv_flat.reshape(ROWS, 3 * D), gate_flat.reshape(ROWS, H), gains_rows)
        a_z = gather_z(shard_a)
        parts_a = gather_rest(a_z[:, :, :half], 1, 2)
        parts_b = gather_rest(a_z[:, :, half:], 2, 1)
        f_up = jnp.concatenate(
            [
                out_flat.reshape(1, ROWS, D),
                up_flat.reshape(ROWS, 4, D).transpose(1, 0, 2),
            ]
        )
        f_all = jnp.concatenate([f_up.reshape(5 * ROWS, D), down_flat.reshape(64, D)])
        f_z = gather_z(f_all)
        parts_u = gather_rest(f_z[:, : 5 * ROWS].reshape(4, 5, ROWS, D), 1, 2)
        parts_d = gather_rest(f_z[:, 5 * ROWS :], 2, 1)
    else:
        whole = [
            lax.all_gather(v, AXES, axis=0, tiled=True)
            for v in (qkv_flat, out_flat, norm_gains, gate_flat, up_flat, down_flat)
        ]
        gains_rows = jnp.repeat(whole[2].reshape(PIECES, GLEN), ROWS, axis=0)
        ext = ext_rows(whole[0].reshape(D, 3 * D), whole[3].reshape(D, H), gains_rows)
        ext = ext.reshape(PIECES, ROWS, EXT)
        parts_a = (ext[:, :, :half],)
        parts_b = (ext[:, :, half:],)
        f_up = jnp.concatenate(
            [
                whole[1].reshape(PIECES, 1, ROWS, D),
                whole[4].reshape(PIECES, ROWS, 4, D).transpose(0, 2, 1, 3),
            ],
            axis=1,
        )
        parts_u = (f_up,)
        parts_d = (whole[5].reshape(PIECES, 64, D),)
    owner_x = owner_fn(split, True)
    owner_y = owner_fn(split, False)

    bias = pl.pallas_call(
        bias_kernel,
        out_shape=jax.ShapeDtypeStruct((3, SEG, SEG), F32),
        name="masks",
    )(doc_row, doc_col, slots)

    (
        qkvt,
        vtok,
        hidt,
        w_ext,
        gatet,
        gains,
        probs,
        local_t,
        mem_t,
        inv_sums,
        mixed_t,
        mixed,
    ) = attention_forward(inputs, bias, parts_a, parts_b, (owner_x, owner_y))
    outs = ffn(
        inputs, cotangent, mixed, mixed_t, gains, parts_u, parts_d, owner_x, owner_y, split
    )
    layer_out, d_resid, dmix_t, dgain_two = outs[:4]
    if split:
        up_keep, up_send, dn_keep, dn_send = outs[4:]
        up_sum = reduce_bit(reduce_bit(reduce_core(up_keep, up_send), 2), 1)
        dn_sum = reduce_bit(reduce_bit(reduce_core(dn_keep, dn_send), 1), 2)
        f_sum = reduce_z(
            jnp.concatenate([up_sum.reshape(4, 5 * ROWS, D), dn_sum], axis=1)
        )
        grad_out = f_sum[:ROWS].reshape(-1)
        grad_up = f_sum[ROWS : 5 * ROWS].reshape(4, ROWS, D).transpose(1, 0, 2).reshape(-1)
        grad_down = f_sum[5 * ROWS :].reshape(-1)
    grad_outs = attention_backward(
        inputs,
        d_resid,
        dgain_two,
        gains,
        gatet,
        w_ext,
        hidt,
        probs,
        local_t,
        mem_t,
        inv_sums,
        dmix_t,
        qkvt,
        vtok,
        owner_x,
        split,
    )
    grad_input = grad_outs[0]
    if split:
        total = reduce_core(grad_outs[1], grad_outs[2])
        ext_sum = reduce_z(reduce_bit(reduce_bit(total, 2), 1))
        grad_qkv = ext_sum[:, : 3 * D].reshape(-1)
        grad_gate = ext_sum[:, 3 * D : 3 * D + H].reshape(-1)
        grad_gains = ext_sum[0, 3 * D + GCOL : 3 * D + GCOL + GLEN]
    else:

        def scatter(v):
            return lax.psum_scatter(
                v.astype(F32).reshape(-1), AXES, scatter_dimension=0, tiled=True
            )

        grad_out = scatter(outs[4][:, 0])
        grad_up = scatter(outs[4][:, 1:].transpose(0, 2, 1, 3))
        grad_down = scatter(outs[5])
        ext = grad_outs[1]
        grad_qkv = scatter(ext[:, :, : 3 * D])
        grad_gate = scatter(ext[:, :, 3 * D : 3 * D + H])
        grad_gains = scatter(ext[:, 0, 3 * D + GCOL : 3 * D + GCOL + GLEN])
    return (layer_out, grad_input, grad_qkv, grad_out, grad_gains, grad_gate, grad_up, grad_down)


def solution(mesh):
    n = mesh.shape["dp"] * mesh.shape["fsdp"]

    def per_device(*args):
        return local(n, *args)

    rows = P(AXES, None)
    flat = P(AXES)
    return jax.shard_map(
        per_device,
        mesh=mesh,
        in_specs=(rows, rows, rows, P(AXES, None, None), flat, flat, flat, flat, flat, flat),
        out_specs=(rows, rows, flat, flat, flat, flat, flat, flat),
        check_vma=False,
    )
```

```python
import jax
import jax.numpy as jnp
from jax import lax
from jax.experimental import pallas as pl
from jax.experimental.pallas import tpu as pltpu
from jax.sharding import PartitionSpec as P

D = 512
H = 8
HD = 64
K = 4
FF = 2048
SEQ = 1024
SEG = 512
PIECES = 32
ROWS = D // PIECES
EXT = 3 * D + 128
GCOL = 8
GLEN = 2 * D // PIECES
NEG = -1e30
BF = jnp.bfloat16
F32 = jnp.float32
AXES = ("dp", "fsdp")
NT = (((1,), (1,)), ((), ()))
TN = (((0,), (0,)), ((), ()))
ANY = pl.BlockSpec(memory_space=pl.ANY)
VLIMIT = 60 * 1024 * 1024


def mm(a, b):
    return jnp.dot(a, b, preferred_element_type=F32)


def mm_nt(a, b):
    return lax.dot_general(a, b, NT, preferred_element_type=F32)


def mm_tn(a, b):
    return lax.dot_general(a, b, TN, preferred_element_type=F32)


def perm_z(v, shift):
    return lax.ppermute(v, "dp", [(i, (i + 4 * shift) % 16) for i in range(16)])


def perm_bit(v, bit):
    return lax.ppermute(v, "dp", [(i, i ^ bit) for i in range(16)])


def perm_core(v):
    return lax.ppermute(v, "fsdp", [(0, 1), (1, 0)])


def after(values, *others):
    done = lax.optimization_barrier((tuple(values), tuple(others)))
    return done[0]


def gather_z(shard):
    return jnp.stack([shard] + [perm_z(shard, -k) for k in (1, 2, 3)])


def gather_plane(stacked):
    return [stacked] + [perm_bit(stacked, bits) for bits in (1, 2, 3)]


def gather_core(parts):
    return list(parts) + [perm_core(part) for part in parts]


def add(keep, got):
    return keep.astype(F32) + got.astype(F32)


def add_z(total):
    out = total[0]
    for k in (1, 2, 3):
        out = out + perm_z(total[k].astype(BF), k).astype(F32)
    return out


def owner_fn(relative, x_first):
    def owner(piece):
        place = lax.axis_index("dp")
        z, y, x = place >> 2, (place >> 1) & 1, place & 1
        kz, low, high, kc = piece & 3, (piece >> 2) & 1, (piece >> 3) & 1, piece >> 4
        kx, ky = (low, high) if x_first else (high, low)
        chip = ((((z + kz) & 3) * 2 + (y ^ ky)) * 2) + (x ^ kx)
        return chip * 2 + (lax.axis_index("fsdp") ^ kc)

    return owner if relative else (lambda piece: piece)


def bias_kernel(doc_row, doc_col, slots, bias):
    sources = lax.broadcasted_iota(jnp.int32, (SEG, SEG), 0)
    places = lax.broadcasted_iota(jnp.int32, (SEG, SEG), 1)
    for seg in range(2):
        part = slice(seg * SEG, (seg + 1) * SEG)
        same = doc_col[part, :] == doc_row[:, part]
        bias[seg] = jnp.where((sources <= places) & same, 0.0, NEG)
    count = jnp.zeros((SEG, SEG), F32)
    for c in range(K):
        count = count + jnp.where(sources == slots[c : c + 1, :], 1.0, 0.0)
    kept = (doc_col[0:SEG, :] == doc_row[:, SEG : 2 * SEG]) & (count > 0.0)
    bias[2] = jnp.where(kept, jnp.log(jnp.maximum(count, 1.0)), NEG)


def rows_from_ext(ext):
    pick = lax.broadcasted_iota(jnp.int32, (PIECES, D), 1) == ROWS * lax.broadcasted_iota(
        jnp.int32, (PIECES, D), 0
    )
    gains = mm(pick.astype(BF), ext).astype(BF)
    source = lax.broadcasted_iota(jnp.int32, (128, D), 0) - GCOL
    column = lax.broadcasted_iota(jnp.int32, (128, D), 1)
    spread = mm(gains, (source == (column & (GLEN - 1))).astype(BF))
    piece = lax.broadcasted_iota(jnp.int32, (PIECES, D), 0)
    block = lax.broadcasted_iota(jnp.int32, (PIECES, D), 1) // GLEN
    one = jnp.sum(jnp.where(block == piece, spread, 0.0), axis=0, keepdims=True)
    two = jnp.sum(jnp.where(block + D // GLEN == piece, spread, 0.0), axis=0, keepdims=True)
    return one, two


def ext_from_gains(column, gain, two):
    row_id = lax.broadcasted_iota(jnp.int32, (D, 128), 0)
    lane = lax.broadcasted_iota(jnp.int32, (D, 128), 1) - GCOL
    target = (lane == (row_id & (GLEN - 1))).astype(BF)
    piece = lax.broadcasted_iota(jnp.int32, (PIECES, D), 0)
    block = lax.broadcasted_iota(jnp.int32, (PIECES, D), 1) // GLEN
    gain_rows = jnp.where(block == piece, 1.0 / gain, 0.0)
    one = lax.dot_general(
        gain_rows,
        jnp.where(lane == (row_id & (GLEN - 1)), column, 0.0),
        (((1,), (0,)), ((), ())),
        precision=lax.Precision.HIGHEST,
        preferred_element_type=F32,
    )
    laid = jnp.where(block + D // GLEN == piece, two, 0.0)
    packed = (one + mm(laid.astype(BF), target)).astype(BF)
    pick = lax.broadcasted_iota(jnp.int32, (D, PIECES), 0) == ROWS * lax.broadcasted_iota(
        jnp.int32, (D, PIECES), 1
    )
    return mm(pick.astype(BF), packed)


def start_pieces(parts, owner, make):
    base = 0
    for part in parts:
        for i in range(part.shape[0]):
            make(part.at[i], owner(base + i)).start()
        base += part.shape[0]


def head_half(rows, upper_half):
    blank = jnp.zeros_like(rows)
    return jnp.concatenate([blank, rows] if upper_half else [rows, blank], axis=0)


PROB_ROWS = 2 * 768 + 1024


def params():
    return pltpu.CompilerParams(vmem_limit_bytes=VLIMIT)


def shape(*dims, dtype=BF):
    return jax.ShapeDtypeStruct(dims, dtype)


def block_rows(d, size):
    return pl.ds(pl.multiple_of(d * size, size), size)


SPOTS = [(seg, ib) for seg in range(3) for ib in range(2)]


def spot(seg, ib):
    key_first = SEG if seg == 1 else 0
    key_count = SEG if seg == 2 else 256 * (ib + 1)
    column = (0 if seg == 0 else SEG) + 256 * ib
    base = 768 * seg + ib * (SEG if seg == 2 else 256)
    return key_first, key_count, column, base


def attention_kernel(owner, count, *refs):
    x_hbm, bias_hbm = refs[:2]
    parts = refs[2 : 2 + count]
    (
        w_o,
        vtok_o,
        qkvt_o,
        hidt_o,
        gatet,
        gains,
        probs,
        local_t,
        mem_t,
        inv_sums,
        mixed_t,
        x,
        bias,
        w,
        ktok,
        vtok,
        qkvt,
        hidt,
        in_sem,
        out_sem,
    ) = refs[2 + count :]
    pair = pl.program_id(0)
    late_out = [(w, w_o), (vtok, vtok_o), (qkvt, qkvt_o), (hidt, hidt_o)]

    @pl.when(pair == 0)
    def _():
        start_pieces(
            parts,
            owner,
            lambda src, d: pltpu.make_async_copy(src, w.at[block_rows(d, ROWS)], in_sem.at[0]),
        )
        pltpu.make_async_copy(x_hbm, x, in_sem.at[1]).start()
        pltpu.make_async_copy(bias_hbm, bias, in_sem.at[2]).start()
        pltpu.make_async_copy(w_o, w, in_sem.at[0]).wait()
        pltpu.make_async_copy(x_hbm, x, in_sem.at[1]).wait()
        g_one, g_two = rows_from_ext(w[:, 3 * D :])
        gains[...] = jnp.concatenate([g_one, g_two], axis=0)
        for block in range(4):
            rows = slice(256 * block, 256 * block + 256)
            xf = x[rows, :].astype(F32)
            factor = lax.rsqrt(jnp.mean(xf * xf, axis=1, keepdims=True) + 1e-06)
            hid = (xf * factor * g_one).astype(BF)
            hidt[:, rows] = hid.T
            query = mm(hid, w[:, 0:D]).astype(BF) * 0.125
            qkvt[0:D, rows] = query.T
            key = mm(hid, w[:, D : 2 * D]).astype(BF)
            ktok[rows, :] = key
            value = mm(hid, w[:, 2 * D : 3 * D]).astype(BF)
            vtok[rows, :] = value
            qkvt[D : 2 * D, rows] = key.T
            qkvt[2 * D : 3 * D, rows] = value.T
            gatet[:, rows] = jax.nn.sigmoid(mm(hid, w[:, 3 * D :])).T[0:H, :]
        for i, (src, dst) in enumerate(late_out):
            pltpu.make_async_copy(src, dst, out_sem.at[i]).start()
        pltpu.make_async_copy(bias_hbm, bias, in_sem.at[2]).wait()

    lanes = block_rows(pair, 128)
    gates = [gatet[pl.ds(2 * pair + hh, 1), :] for hh in range(2)]

    def head_rows(third, hh, first, count):
        start = pl.multiple_of(third * D + pair * 128 + hh * HD, HD)
        return qkvt[pl.ds(start, HD), first : first + count]

    def scores(hh, seg, ib):
        key_first, key_count, column, base = spot(seg, ib)
        query = head_half(head_rows(0, hh, column, 256), hh)
        return mm(ktok[key_first : key_first + key_count, lanes], query)

    def soft(score, hh, seg, ib):
        key_first, key_count, column, base = spot(seg, ib)
        score = score + bias[seg, 0:key_count, 256 * ib : 256 * ib + 256]
        peak = jnp.max(score, axis=0, keepdims=True)
        if seg == 2:
            peak = jnp.maximum(peak, 0.0)
        expo = jnp.exp(score - peak)
        total = jnp.sum(expo, axis=0, keepdims=True)
        if seg == 2:
            total = total + jnp.exp(-peak)
        expo_b = expo.astype(BF)
        probs[0, hh, base : base + key_count, :] = expo_b
        return expo_b, 1.0 / total

    held = {}

    def close(expo_b, inverse, hh, seg, ib):
        key_first, key_count, column, base = spot(seg, ib)
        rows = slice(hh * HD, (hh + 1) * HD)
        found = mm(head_rows(2, hh, key_first, key_count), expo_b) * inverse
        here = gates[hh][:, column : column + 256]
        if seg < 2:
            local_t[rows, column : column + 256] = found.astype(BF)
            inv_sums[0, hh : hh + 1, column : column + 256] = inverse
            if seg == 0:
                mixed_t[rows, column : column + 256] = (here * found).astype(BF)
            else:
                held[hh, ib] = here * found
            return
        mem_t[rows, 256 * ib : 256 * ib + 256] = found.astype(BF)
        inv_sums[0, 2 + hh : 3 + hh, 256 * ib : 256 * ib + 256] = inverse
        mixed_t[rows, column : column + 256] = (
            held.pop((hh, ib)) + (1.0 - here) * found
        ).astype(BF)

    order = [(hh, seg, ib) for ib in range(2) for seg in range(3) for hh in range(2)]
    waiting = scores(*order[0])
    late = None
    for i, item in enumerate(order):
        score = waiting
        if i + 1 < len(order):
            waiting = scores(*order[i + 1])
        expo_b, inverse = soft(score, *item)
        if late is not None:
            close(*late)
        late = (expo_b, inverse) + item
    close(*late)
    inv_sums[0, 2:4, SEG:] = jnp.zeros((2, SEG), F32)

    @pl.when(pair == 3)
    def _():
        for i, (src, dst) in enumerate(late_out):
            pltpu.make_async_copy(src, dst, out_sem.at[i]).wait()


def attention(x, bias, parts, owner, deps=()):
    count_in = 2 + len(parts)

    def body(*refs):
        attention_kernel(owner, len(parts), *refs[:count_in], *refs[count_in + len(deps) :])

    const2 = lambda p: (0, 0)
    down = lambda p: (p, 0)
    return pl.pallas_call(
        body,
        grid=(4,),
        in_specs=[ANY] * (count_in + len(deps)),
        out_specs=[
            ANY,
            ANY,
            ANY,
            ANY,
            pl.BlockSpec((H, SEQ), const2),
            pl.BlockSpec((2, D), const2),
            pl.BlockSpec((1, 2, PROB_ROWS, 256), lambda p: (p, 0, 0, 0)),
            pl.BlockSpec((128, SEQ), down),
            pl.BlockSpec((128, SEG), down),
            pl.BlockSpec((1, 4, SEQ), lambda p: (p, 0, 0)),
            pl.BlockSpec((128, SEQ), down),
        ],
        out_shape=[
            shape(D, EXT),
            shape(SEQ, D),
            shape(3 * D, SEQ),
            shape(D, SEQ),
            shape(H, SEQ, dtype=F32),
            shape(2, D, dtype=F32),
            shape(4, 2, PROB_ROWS, 256),
            shape(D, SEQ),
            shape(D, SEG),
            shape(4, 4, SEQ, dtype=F32),
            shape(D, SEQ),
        ],
        scratch_shapes=[
            pltpu.VMEM((SEQ, D), BF),
            pltpu.VMEM((3, SEG, SEG), F32),
            pltpu.VMEM((D, EXT), BF),
            pltpu.VMEM((SEQ, D), BF),
            pltpu.VMEM((SEQ, D), BF),
            pltpu.VMEM((3 * D, SEQ), BF),
            pltpu.VMEM((D, SEQ), BF),
            pltpu.SemaphoreType.DMA((3,)),
            pltpu.SemaphoreType.DMA((4,)),
        ],
        compiler_params=params(),
        cost_estimate=pl.CostEstimate(
            flops=18_000_000_000, bytes_accessed=40_000_000, transcendentals=6_000_000
        ),
        name="attention",
    )(x, bias, *parts, *deps)


TILE = 256
TILES = FF // TILE


def ffn_kernel(owner_u, owner_d, count, count_o, *refs):
    x_hbm, cot_hbm, mixt_hbm, gains = refs[:4]
    parts_u = refs[4 : 4 + count]
    parts_d = refs[4 + count : 4 + 2 * count]
    refs = refs[4 + 2 * count :]
    layer_o, d_resid_o, dmix_o, dgain = refs[:4]
    grads_u = refs[4 : 4 + count_o]
    grads_d = refs[4 + count_o : 4 + 2 * count_o]
    (
        x,
        cot,
        mixt,
        w_out,
        w_up,
        w_dn,
        hid,
        hidt,
        resid,
        oacc,
        dacc,
        dmix,
        g_out,
        g_up,
        g_dn,
        held_up,
        held_act,
        acts,
        d_ups,
        factors,
        in_sem,
        out_sem,
    ) = refs[4 + 2 * count_o :]
    per = PIECES // count_o

    def lanes_of(tile):
        return pl.ds(pl.multiple_of((tile % 2) * TILE, TILE), TILE)

    def up_tile(tile):
        return w_up[tile // 2, :, lanes_of(tile)]

    def dn_tile(tile):
        return w_dn[pl.ds(tile * (TILE // ROWS), TILE // ROWS)].reshape(TILE, D)

    def head_up(tile, slot):
        held_up[slot] = mm(hid[...], up_tile(tile))

    def head_act(tile, slot):
        held_act[slot] = mm_nt(cot[...], dn_tile(tile))

    def head(tile, slot):
        head_up(tile, slot)
        head_act(tile, slot)

    def gelu(slot, first, last):
        c0 = 0.7978845608028654
        c1 = 0.044715
        for block in range(first, last):
            rows = slice(64 * block, 64 * block + 64)
            upper = held_up[slot, rows, :]
            square = upper * upper
            tanh = jnp.tanh(upper * (c0 + (c0 * c1) * square))
            half_t = 0.5 * tanh + 0.5
            slope = half_t + upper * (1.0 - tanh * tanh) * (0.5 * c0 + (1.5 * c0 * c1) * square)
            acts[slot, rows, :] = (upper * half_t).astype(BF)
            d_ups[slot, rows, :] = (held_act[slot, rows, :] * slope).astype(BF)

    def tail_out(tile, slot):
        oacc[...] += mm(acts[slot], dn_tile(tile))

    def tail_hid(tile, slot):
        dacc[...] += mm_nt(d_ups[slot], up_tile(tile))

    def tail_dn(tile, slot):
        g_dn[pl.ds(tile * (TILE // ROWS), TILE // ROWS)] = (
            mm_tn(acts[slot], cot[...]).astype(BF).reshape(TILE // ROWS, ROWS, D)
        )

    def tail_up(tile, slot):
        g_up[tile // 2, :, lanes_of(tile)] = mm(hidt[...], d_ups[slot]).astype(BF)

    def tail(tile, slot):
        tail_out(tile, slot)
        tail_hid(tile, slot)
        tail_dn(tile, slot)
        tail_up(tile, slot)

    def spread(step, now):
        later = jnp.minimum(step + 1, TILES - 1)
        before = jnp.maximum(step - 1, 0)
        jobs = (tail_dn, tail_out, head_up, tail_up, tail_hid, head_act)
        count = 16
        for i, job in enumerate(jobs):
            gelu(now, count * i // 6, count * (i + 1) // 6)
            job(later if job in (head_up, head_act) else before, 1 - now)

    start_pieces(
        parts_u,
        owner_u,
        lambda src, d: pltpu.make_async_copy(
            src.at[0], w_out.at[block_rows(d, ROWS), :], in_sem.at[0]
        ),
    )
    pltpu.make_async_copy(mixt_hbm, mixt, in_sem.at[4]).start()
    pltpu.make_async_copy(x_hbm, x, in_sem.at[5]).start()
    start_pieces(
        parts_u,
        owner_u,
        lambda src, d: pltpu.make_async_copy(
            src.at[pl.ds(1, 4)], w_up.at[:, block_rows(d, ROWS), :], in_sem.at[1]
        ),
    )
    start_pieces(
        parts_d,
        owner_d,
        lambda src, d: pltpu.make_async_copy(src, w_dn.at[pl.ds(d * 4, 4)], in_sem.at[2]),
    )
    pltpu.make_async_copy(cot_hbm, cot, in_sem.at[3]).start()
    pltpu.make_async_copy(g_out, w_out, in_sem.at[0]).wait()
    pltpu.make_async_copy(mixt_hbm, mixt, in_sem.at[4]).wait()
    pltpu.make_async_copy(x_hbm, x, in_sem.at[5]).wait()
    dacc[...] = jnp.zeros_like(dacc)
    acts[1] = jnp.zeros((SEQ, TILE), BF)
    d_ups[1] = jnp.zeros((SEQ, TILE), BF)
    for block in range(4):
        rows = slice(256 * block, 256 * block + 256)
        value = x[rows, :].astype(F32) + mm_tn(mixt[:, rows], w_out[...])
        factor = lax.rsqrt(jnp.mean(value * value, axis=1, keepdims=True) + 1e-06)
        normed = (value * factor * gains[1:2, :]).astype(BF)
        factors[rows, :] = factor
        resid[rows, :] = value
        oacc[rows, :] = value
        hid[rows, :] = normed
        hidt[:, rows] = normed.T
    pltpu.make_async_copy(g_up, w_up, in_sem.at[1]).wait()
    pltpu.make_async_copy(g_dn, w_dn, in_sem.at[2]).wait()
    pltpu.make_async_copy(cot_hbm, cot, in_sem.at[3]).wait()
    head(0, 0)

    @pl.loop(0, TILES)
    def _(step):
        spread(step, step % 2)

    tail(TILES - 1, (TILES - 1) % 2)
    for piece in range(PIECES):
        pltpu.make_async_copy(
            g_up.at[:, block_rows(owner_u(piece), ROWS), :],
            grads_u[piece // per].at[piece % per, pl.ds(1, 4)],
            out_sem.at[0],
        ).start()
        pltpu.make_async_copy(
            g_dn.at[pl.ds(owner_d(piece) * 4, 4)],
            grads_d[piece // per].at[piece % per],
            out_sem.at[1],
        ).start()
    g_two = gains[1:2, :]
    total = jnp.zeros((1, D), F32)
    for block in range(16):
        rows = slice(64 * block, 64 * block + 64)
        value = resid[rows, :]
        factor = factors[rows, :]
        d_hid = dacc[rows, :]
        product = d_hid * value
        total = total + jnp.sum(product * factor, axis=0, keepdims=True)
        inner = jnp.mean(product * g_two, axis=1, keepdims=True)
        d_resid = cot[rows, :].astype(F32) + (
            factor * (d_hid * g_two) - value * (factor * factor * factor * inner)
        )
        x[rows, :] = oacc[rows, :].astype(BF)
        resid[rows, :] = d_resid
        hid[rows, :] = d_resid.astype(BF)
    dgain[...] = total
    pltpu.make_async_copy(x, layer_o, out_sem.at[2]).start()
    pltpu.make_async_copy(resid, d_resid_o, out_sem.at[3]).start()
    g_out[...] = mm(mixt[...], hid[...]).astype(BF)
    for piece in range(PIECES):
        pltpu.make_async_copy(
            g_out.at[block_rows(owner_u(piece), ROWS), :],
            grads_u[piece // per].at[piece % per, 0],
            out_sem.at[5],
        ).start()
    dmix[...] = mm_nt(w_out[...], hid[...]).astype(BF)
    pltpu.make_async_copy(dmix, dmix_o, out_sem.at[4]).start()
    pltpu.make_async_copy(g_up, w_up, out_sem.at[0]).wait()
    pltpu.make_async_copy(g_dn, w_dn, out_sem.at[1]).wait()
    pltpu.make_async_copy(x, layer_o, out_sem.at[2]).wait()
    pltpu.make_async_copy(resid, d_resid_o, out_sem.at[3]).wait()
    pltpu.make_async_copy(g_out, w_out, out_sem.at[5]).wait()
    pltpu.make_async_copy(dmix, dmix_o, out_sem.at[4]).wait()


def ffn(x, cot, mixed_t, gains, parts_u, parts_d, owner_u, owner_d, count_o):
    def body(*refs):
        ffn_kernel(owner_u, owner_d, len(parts_u), count_o, *refs)

    return pl.pallas_call(
        body,
        in_specs=[ANY, ANY, ANY, pl.BlockSpec(memory_space=pltpu.VMEM)]
        + [ANY] * (len(parts_u) + len(parts_d)),
        out_specs=[ANY, ANY, ANY, pl.BlockSpec(memory_space=pltpu.VMEM)] + [ANY] * (2 * count_o),
        out_shape=[
            shape(SEQ, D),
            shape(SEQ, D, dtype=F32),
            shape(D, SEQ),
            shape(1, D, dtype=F32),
        ]
        + [shape(PIECES // count_o, 5, ROWS, D)] * count_o
        + [shape(PIECES // count_o, 4, ROWS, D)] * count_o,
        scratch_shapes=[
            pltpu.VMEM((SEQ, D), BF),
            pltpu.VMEM((SEQ, D), BF),
            pltpu.VMEM((D, SEQ), BF),
            pltpu.VMEM((D, D), BF),
            pltpu.VMEM((4, D, D), BF),
            pltpu.VMEM((FF // ROWS, ROWS, D), BF),
            pltpu.VMEM((SEQ, D), BF),
            pltpu.VMEM((D, SEQ), BF),
            pltpu.VMEM((SEQ, D), F32),
            pltpu.VMEM((SEQ, D), F32),
            pltpu.VMEM((SEQ, D), F32),
            pltpu.VMEM((D, SEQ), BF),
            pltpu.VMEM((D, D), BF),
            pltpu.VMEM((4, D, D), BF),
            pltpu.VMEM((FF // ROWS, ROWS, D), BF),
            pltpu.VMEM((2, SEQ, TILE), F32),
            pltpu.VMEM((2, SEQ, TILE), F32),
            pltpu.VMEM((2, SEQ, TILE), BF),
            pltpu.VMEM((2, SEQ, TILE), BF),
            pltpu.VMEM((SEQ, 1), F32),
            pltpu.SemaphoreType.DMA((6,)),
            pltpu.SemaphoreType.DMA((6,)),
        ],
        compiler_params=params(),
        cost_estimate=pl.CostEstimate(
            flops=25_000_000_000, bytes_accessed=25_000_000, transcendentals=2_000_000
        ),
        name="feed_forward",
    )(x, cot, mixed_t, gains, *parts_u, *parts_d)


def attention_back_kernel(first, last, owner, count_o, *refs):
    (gatet, w_hbm, hidt_hbm, probs, local_t, mem_t, inv_sums, dmix_t, qt, kt, vtok) = refs[:11]
    refs = refs[11:]
    if last:
        gains, dgain_two, before, gates_before, grad_before = refs[:5]
        refs = refs[5:]
    else:
        count_o = 1
    dqkvt, d_gates, *refs = refs
    if not last:
        weighted = refs[0]
        refs = refs[1:]
    grads = refs[:count_o]
    w, hidt, scratch, gate_rows, g_ext, in_sem, out_sem = refs[count_o:]
    pair = pl.program_id(0)
    per = PIECES // count_o

    def before_columns(third):
        return pltpu.make_async_copy(
            grad_before.at[third], g_ext.at[:, pl.ds(third * D, 256)], in_sem.at[2]
        )

    @pl.when(pair == 0)
    def _():
        pltpu.make_async_copy(hidt_hbm, hidt, in_sem.at[0]).start()
        pltpu.make_async_copy(w_hbm, w, in_sem.at[1]).start()
        if last:
            for third in range(3):
                before_columns(third).start()

    ups = {}
    dots = {}
    for hh in range(2):
        rows = slice(hh * HD, (hh + 1) * HD)
        gate = gatet[pl.ds(2 * (first + pair) + hh, 1), :]
        d_mix = dmix_t[rows, :].astype(F32)
        local = local_t[rows, :].astype(F32)
        mem = mem_t[rows, :].astype(F32)
        inv_local = inv_sums[0, hh : hh + 1, :]
        inv_mem = inv_sums[0, 2 + hh : 3 + hh, 0:SEG]
        d_local = (d_mix * (gate * inv_local)).astype(BF)
        d_mem = (d_mix[:, SEG:] * ((1.0 - gate[:, SEG:]) * inv_mem)).astype(BF)
        dot_local = jnp.sum(d_local.astype(F32) * local, axis=0, keepdims=True)
        dot_mem = jnp.sum(d_mem.astype(F32) * mem, axis=0, keepdims=True)
        plain_local = jnp.sum(d_mix * local, axis=0, keepdims=True)
        plain_mem = jnp.sum(d_mix[:, SEG:] * mem, axis=0, keepdims=True)
        d_gate = gate * (1.0 - gate) * (
            plain_local - jnp.concatenate([jnp.zeros((1, SEG), F32), plain_mem], axis=1)
        )
        d_gates[0, hh : hh + 1, :] = d_gate
        gate_rows[pl.ds(2 * pair + hh, 1), :] = d_gate
        for seg, ib in SPOTS:
            column = spot(seg, ib)[2]
            if seg == 2:
                ups[hh, seg, ib] = d_mem[:, 256 * ib : 256 * ib + 256]
                dots[hh, seg, ib] = dot_mem[:, 256 * ib : 256 * ib + 256]
            else:
                ups[hh, seg, ib] = d_local[:, column : column + 256]
                dots[hh, seg, ib] = dot_local[:, column : column + 256]

    sums_of = {}

    def add(key, value):
        sums_of[key] = value if key not in sums_of else sums_of[key] + value

    def begin(hh, seg, ib):
        key_first, key_count, column, base = spot(seg, ib)
        return mm(vtok[key_first : key_first + key_count, :], head_half(ups[hh, seg, ib], hh))

    def middle(d_prob, hh, seg, ib):
        key_first, key_count, column, base = spot(seg, ib)
        expo = probs[0, hh, base : base + key_count, :]
        return (expo.astype(F32) * (d_prob - dots[hh, seg, ib])).astype(BF), expo

    def close(d_score, expo, hh, seg, ib):
        key_first, key_count, column, base = spot(seg, ib)
        rows = slice(hh * HD, (hh + 1) * HD)
        add((0, hh, column // 256), mm(kt[rows, key_first : key_first + key_count], d_score))
        key_term = mm_nt(qt[rows, column : column + 256], d_score)
        value_term = mm_nt(ups[hh, seg, ib], expo)
        for part in range(key_count // 256):
            place = key_first // 256 + part
            add((1, hh, place), key_term[:, 256 * part : 256 * part + 256])
            add((2, hh, place), value_term[:, 256 * part : 256 * part + 256])

    order = [(hh, seg, ib) for seg in (0, 2, 1) for ib in range(2) for hh in range(2)]
    waiting = begin(*order[0])
    late = None
    for i, item in enumerate(order):
        d_prob = waiting
        if i + 1 < len(order):
            waiting = begin(*order[i + 1])
        d_score, expo = middle(d_prob, *item)
        if late is not None:
            close(*late)
        late = (d_score, expo) + item
    close(*late)
    for (third, hh, place), value in sums_of.items():
        if third == 0:
            value = value * 0.125
        rows = slice(hh * HD, (hh + 1) * HD)
        dqkvt[third, rows, 256 * place : 256 * place + 256] = value.astype(BF)
    scratch[:, block_rows(pair, 128), :] = dqkvt[...]

    @pl.when(pair == 1)
    def _():
        pltpu.make_async_copy(hidt_hbm, hidt, in_sem.at[0]).wait()
        pltpu.make_async_copy(w_hbm, w, in_sem.at[1]).wait()
        sums = jnp.zeros((D, 128), F32)
        for third in range(3):
            grad = mm_nt(hidt[...], scratch[third])
            start = third * D + first * 128
            for part in range(2):
                columns = slice(start + 128 * part, start + 128 * part + 128)
                sums = sums + grad[:, 128 * part : 128 * part + 128] * w[:, columns].astype(F32)
            if last:
                g_ext[:, third * D + 256 : third * D + 512] = grad.astype(BF)
            else:
                g_ext[third] = grad.astype(BF)
        if last:
            d_gate_b = jnp.concatenate(
                [
                    gates_before[0],
                    gates_before[1],
                    gate_rows[0:4, :],
                    jnp.zeros((120, SEQ), F32),
                ],
                axis=0,
            ).astype(BF)
            grad = mm_nt(hidt[...], d_gate_b)
            gate_lane = lax.broadcasted_iota(jnp.int32, (D, 128), 1) < H
            sums = sums + before[...] + jnp.where(
                gate_lane, grad * w[:, 3 * D :].astype(F32), 0.0
            )
            column = jnp.sum(sums, axis=1, keepdims=True)
            g_ext[:, 3 * D :] = (grad + ext_from_gains(column, gains[0:1, :], dgain_two[...])).astype(
                BF
            )
        if not last:
            weighted[...] = sums
            pltpu.make_async_copy(g_ext, grads[0], out_sem).start()
            pltpu.make_async_copy(g_ext, grads[0], out_sem).wait()
        else:
            for third in range(3):
                before_columns(third).wait()
            for piece in range(PIECES):
                pltpu.make_async_copy(
                    g_ext.at[block_rows(owner(piece), ROWS), :],
                    grads[piece // per].at[piece % per],
                    out_sem,
                ).start()
            pltpu.make_async_copy(w, g_ext, out_sem).wait()


def attention_back(
    first, gatet, w, hidt, saved, dmix_t, qkvt, vtok, owner, count_o, extra=(), deps=()
):
    last = len(extra) > 0
    const2 = lambda p: (0, 0)
    count_in = 11 + len(extra)

    def body(*refs):
        attention_back_kernel(
            first, last, owner, count_o, *refs[:count_in], *refs[count_in + len(deps) :]
        )

    extra_specs = []
    if last:
        extra_specs = [
            pl.BlockSpec((2, D), const2),
            pl.BlockSpec((1, D), const2),
            pl.BlockSpec((D, 128), const2),
            pl.BlockSpec((2, 2, SEQ), lambda p: (0, 0, 0)),
            ANY,
        ]
    sums_spec = [] if last else [pl.BlockSpec((D, 128), const2)]
    sums_shape = [] if last else [shape(D, 128, dtype=F32)]
    return pl.pallas_call(
        body,
        grid=(2,),
        in_specs=[
            pl.BlockSpec((H, SEQ), const2),
            ANY,
            ANY,
            pl.BlockSpec((1, 2, PROB_ROWS, 256), lambda p: (first + p, 0, 0, 0)),
            pl.BlockSpec((128, SEQ), lambda p: (first + p, 0)),
            pl.BlockSpec((128, SEG), lambda p: (first + p, 0)),
            pl.BlockSpec((1, 4, SEQ), lambda p: (first + p, 0, 0)),
            pl.BlockSpec((128, SEQ), lambda p: (first + p, 0)),
            pl.BlockSpec((128, SEQ), lambda p: (first + p, 0)),
            pl.BlockSpec((128, SEQ), lambda p: (4 + first + p, 0)),
            pl.BlockSpec((SEQ, 128), lambda p: (0, first + p)),
        ]
        + extra_specs
        + [ANY] * len(deps),
        out_specs=[
            pl.BlockSpec((3, 128, SEQ), lambda p: (0, p, 0)),
            pl.BlockSpec((1, 2, SEQ), lambda p: (p, 0, 0)),
        ]
        + sums_spec
        + [ANY] * (count_o if last else 1),
        out_shape=[shape(3, 256, SEQ), shape(2, 2, SEQ, dtype=F32)]
        + sums_shape
        + ([shape(PIECES // count_o, ROWS, EXT)] * count_o if last else [shape(3, D, 256)]),
        scratch_shapes=[
            pltpu.VMEM((D, EXT), BF),
            pltpu.VMEM((D, SEQ), BF),
            pltpu.VMEM((3, 256, SEQ), BF),
            pltpu.VMEM((8, SEQ), F32),
            pltpu.VMEM((D, EXT) if last else (3, D, 256), BF),
            pltpu.SemaphoreType.DMA((3,)),
            pltpu.SemaphoreType.DMA,
        ],
        compiler_params=params(),
        cost_estimate=pl.CostEstimate(
            flops=11_000_000_000, bytes_accessed=20_000_000, transcendentals=0
        ),
        name="attention_back",
    )(gatet, w, hidt, *saved, dmix_t, qkvt, qkvt, vtok, *extra, *deps)


def input_back_kernel(x, d_resid, gains, w, da, db, gates_a, gates_b, grad_in):
    d_gate = jnp.concatenate(
        [gates_a[0], gates_a[1], gates_b[0], gates_b[1], jnp.zeros((120, 256), F32)], axis=0
    ).astype(BF)
    d_hid = mm(w[:, 3 * D :], d_gate)
    for third in range(3):
        start = third * D
        d_hid = d_hid + mm(w[:, start : start + 256], da[third])
        d_hid = d_hid + mm(w[:, start + 256 : start + 512], db[third])
    d_hid = d_hid.T
    xf = x[...].astype(F32)
    factor = lax.rsqrt(jnp.mean(xf * xf, axis=1, keepdims=True) + 1e-06)
    scaled = d_hid * gains[0:1, :]
    inner = jnp.mean(scaled * xf, axis=1, keepdims=True)
    grad_in[...] = (
        d_resid[...] + factor * scaled - xf * (factor * factor * factor * inner)
    ).astype(BF)


def input_back(x, d_resid, gains, w, da, db, gates_a, gates_b, deps=()):
    def body(*refs):
        input_back_kernel(*refs[:8], refs[-1])

    const2 = lambda i: (0, 0)
    rows = lambda i: (i, 0)
    across = lambda i: (0, 0, i)
    return pl.pallas_call(
        body,
        grid=(4,),
        in_specs=[
            pl.BlockSpec((256, D), rows),
            pl.BlockSpec((256, D), rows),
            pl.BlockSpec((2, D), const2),
            pl.BlockSpec((D, EXT), const2),
            pl.BlockSpec((3, 256, 256), across),
            pl.BlockSpec((3, 256, 256), across),
            pl.BlockSpec((2, 2, 256), across),
            pl.BlockSpec((2, 2, 256), across),
        ]
        + [ANY] * len(deps),
        out_specs=pl.BlockSpec((256, D), rows),
        out_shape=shape(SEQ, D),
        compiler_params=params(),
        cost_estimate=pl.CostEstimate(
            flops=5_000_000_000, bytes_accessed=9_000_000, transcendentals=0
        ),
        name="input_back",
    )(x, d_resid, gains, w, da, db, gates_a, gates_b, *deps)


def ext_rows(qkv, gate, gains):
    count = qkv.shape[0]
    blank = jnp.zeros((count, 128 - GCOL - gains.shape[1]), BF)
    return jnp.concatenate([qkv, gate, gains, blank], axis=1)


def local(
    n, inputs, cotangent, doc_ids, slot_ids, qkv_flat, out_flat, norm_gains, gate_flat, up_flat, down_flat
):
    split = n == PIECES
    count_o = 2 if split else 1
    owner_x = owner_fn(split, True)
    owner_y = owner_fn(split, False)
    doc_row = doc_ids.reshape(1, SEQ)
    doc_col = doc_ids.reshape(SEQ, 1)
    slots = slot_ids.reshape(SEG, K).T
    bias = pl.pallas_call(
        bias_kernel,
        out_shape=shape(3, SEG, SEG, dtype=F32),
        name="masks",
    )(doc_row, doc_col, slots)
    if split:
        gains_rows = jnp.broadcast_to(norm_gains.reshape(1, GLEN), (ROWS, GLEN))
        shard_a = ext_rows(qkv_flat.reshape(ROWS, 3 * D), gate_flat.reshape(ROWS, H), gains_rows)
        z_a = gather_z(shard_a)
        shard_f = jnp.concatenate(
            [
                out_flat.reshape(1, ROWS, D),
                up_flat.reshape(ROWS, 4, D).transpose(1, 0, 2),
                down_flat.reshape(4, ROWS, D),
            ]
        )
        plane_a = after(gather_plane(z_a), bias)
        parts_a = gather_core(plane_a)
        z_f = gather_z(shard_f)
        z_u, z_d = z_f[:, :5], z_f[:, 5:]
        wide_u = jnp.concatenate([z_u, perm_bit(z_u, 1)])
        wide_d = jnp.concatenate([z_d, perm_bit(z_d, 2)])
        halves_u = [wide_u, perm_bit(wide_u, 2)]
        halves_d = [wide_d, perm_bit(wide_d, 1)]
        deps = (wide_u, wide_d)
    else:
        whole = [
            lax.all_gather(v, AXES, axis=0, tiled=True)
            for v in (qkv_flat, out_flat, norm_gains, gate_flat, up_flat, down_flat)
        ]
        gains_rows = jnp.repeat(whole[2].reshape(PIECES, GLEN), ROWS, axis=0)
        ext = ext_rows(whole[0].reshape(D, 3 * D), whole[3].reshape(D, H), gains_rows)
        parts_a = (ext.reshape(PIECES, ROWS, EXT),)
        parts_u = (
            jnp.concatenate(
                [
                    whole[1].reshape(PIECES, 1, ROWS, D),
                    whole[4].reshape(PIECES, ROWS, 4, D).transpose(0, 2, 1, 3),
                ],
                axis=1,
            ),
        )
        parts_d = (whole[5].reshape(PIECES, 4, ROWS, D),)
        deps = ()
    w_ext, vtok, qkvt, hidt, gatet, gains, *saved, mixed_t = attention(
        inputs, bias, parts_a, owner_x, deps
    )
    if split:
        far_u, far_d = after((halves_u[1], halves_d[1]), gatet)
        parts_u = gather_core((wide_u, far_u))
        parts_d = gather_core((wide_d, far_d))
    layer_out, d_resid, dmix_t, dgain_two, *grads_f = ffn(
        inputs, cotangent, mixed_t, gains, parts_u, parts_d, owner_x, owner_y, count_o
    )
    da, gates_a, weighted, grad_before = attention_back(
        0, gatet, w_ext, hidt, saved, dmix_t, qkvt, vtok, owner_x, count_o
    )
    deps = ()
    if split:
        keep_u, send_u, keep_d, send_d = grads_f
        got_u, got_d = after((perm_core(send_u), perm_core(send_d)), gates_a)
        firsts = (
            add(keep_u[:8], got_u[:8]),
            add(keep_u[8:], got_u[8:]).astype(BF),
            add(keep_d[:8], got_d[:8]),
            add(keep_d[8:], got_d[8:]).astype(BF),
        )
        deps = firsts
    db, gates_b, *grads_a = attention_back(
        2,
        gatet,
        w_ext,
        hidt,
        saved,
        dmix_t,
        qkvt,
        vtok,
        owner_x,
        count_o,
        (gains, dgain_two, weighted, gates_a, grad_before),
        deps,
    )
    deps = ()
    if split:
        got_u, got_d = after((perm_bit(firsts[1], 2), perm_bit(firsts[3], 1)), gates_b)
        seconds = (
            add(firsts[0][:4], got_u[:4]),
            add(firsts[0][4:], got_u[4:]).astype(BF),
            add(firsts[2][:4], got_d[:4]),
            add(firsts[2][4:], got_d[4:]).astype(BF),
        )
        keep_a, send_a = grads_a
        got_a = perm_core(send_a)
        sends_a = [
            add(keep_a[4 * k : 4 * k + 4], got_a[4 * k : 4 * k + 4]).astype(BF) for k in (1, 2, 3)
        ]
        deps = (*sends_a, seconds[1], seconds[3])
    grad_input = input_back(inputs, d_resid, gains, w_ext, da, db, gates_a, gates_b, deps)
    if split:
        got_u, got_d = after((perm_bit(seconds[1], 1), perm_bit(seconds[3], 2)), grad_input)
        sum_f = add_z(
            jnp.concatenate([add(seconds[0], got_u), add(seconds[2], got_d)], axis=1)
        )
        total_a = add(keep_a[:4], got_a[:4])
        for k in (1, 2, 3):
            total_a = add(total_a, perm_bit(sends_a[k - 1], k))
        sum_a = add_z(total_a)
        grad_out = sum_f[0].reshape(-1)
        grad_up = sum_f[1:5].transpose(1, 0, 2).reshape(-1)
        grad_down = sum_f[5:].reshape(-1)
        grad_qkv = sum_a[:, : 3 * D].reshape(-1)
        grad_gate = sum_a[:, 3 * D : 3 * D + H].reshape(-1)
        grad_gains = sum_a[0, 3 * D + GCOL : 3 * D + GCOL + GLEN]
    else:

        def scatter(v):
            return lax.psum_scatter(
                v.astype(F32).reshape(-1), AXES, scatter_dimension=0, tiled=True
            )

        grad_out = scatter(grads_f[0][:, 0])
        grad_up = scatter(grads_f[0][:, 1:].transpose(0, 2, 1, 3))
        grad_down = scatter(grads_f[1])
        ext = grads_a[0]
        grad_qkv = scatter(ext[:, :, : 3 * D])
        grad_gate = scatter(ext[:, :, 3 * D : 3 * D + H])
        grad_gains = scatter(ext[:, 0, 3 * D + GCOL : 3 * D + GCOL + GLEN])
    return (layer_out, grad_input, grad_qkv, grad_out, grad_gains, grad_gate, grad_up, grad_down)


def solution(mesh):
    n = mesh.shape["dp"] * mesh.shape["fsdp"]

    def per_device(*args):
        return local(n, *args)

    rows = P(AXES, None)
    flat = P(AXES)
    return jax.shard_map(
        per_device,
        mesh=mesh,
        in_specs=(rows, rows, rows, P(AXES, None, None), flat, flat, flat, flat, flat, flat),
        out_specs=(rows, rows, flat, flat, flat, flat, flat, flat),
        check_vma=False,
    )
```

```python
import jax
import jax.numpy as jnp
from jax import lax
from jax.experimental import pallas as pl
from jax.experimental.pallas import tpu as pltpu
from jax.sharding import PartitionSpec as P

D = 512
H = 8
HD = 64
K = 4
FF = 2048
SEQ = 1024
SEG = 512
PIECES = 32
ROWS = D // PIECES
EXT = 3 * D + 128
GCOL = 8
GLEN = 2 * D // PIECES
NEG = -1e30
EARLY = 1
BF = jnp.bfloat16
F32 = jnp.float32
AXES = ("dp", "fsdp")
NT = (((1,), (1,)), ((), ()))
TN = (((0,), (0,)), ((), ()))
ANY = pl.BlockSpec(memory_space=pl.ANY)


def mm(a, b):
    return jnp.dot(a, b, preferred_element_type=F32)


def mm_nt(a, b):
    return lax.dot_general(a, b, NT, preferred_element_type=F32)


def mm_tn(a, b):
    return lax.dot_general(a, b, TN, preferred_element_type=F32)


def perm_z(v, shift):
    return lax.ppermute(v, "dp", [(i, (i + 4 * shift) % 16) for i in range(16)])


def perm_bit(v, bit):
    return lax.ppermute(v, "dp", [(i, i ^ bit) for i in range(16)])


def perm_core(v):
    return lax.ppermute(v, "fsdp", [(0, 1), (1, 0)])


def after(values, *others):
    done = lax.optimization_barrier((tuple(values), tuple(others)))
    return done[0]


def gather_z(shard):
    return jnp.stack([shard] + [perm_z(shard, -k) for k in (1, 2, 3)])


def gather_plane(stacked):
    return [stacked] + [perm_bit(stacked, bits) for bits in (1, 2, 3)]


def gather_core(parts):
    return list(parts) + [perm_core(part) for part in parts]


def add(keep, got):
    return keep.astype(F32) + got.astype(F32)


def add_z(total):
    out = total[0]
    for k in (1, 2, 3):
        out = out + perm_z(total[k].astype(BF), k).astype(F32)
    return out


def owner_fn(relative, x_first):
    def owner(piece):
        place = lax.axis_index("dp")
        z, y, x = place >> 2, (place >> 1) & 1, place & 1
        kz, low, high, kc = piece & 3, (piece >> 2) & 1, (piece >> 3) & 1, piece >> 4
        kx, ky = (low, high) if x_first else (high, low)
        chip = ((((z + kz) & 3) * 2 + (y ^ ky)) * 2) + (x ^ kx)
        return chip * 2 + (lax.axis_index("fsdp") ^ kc)

    return owner if relative else (lambda piece: piece)


def bias_kernel(doc_row, doc_col, slots, bias):
    sources = lax.broadcasted_iota(jnp.int32, (SEG, SEG), 0)
    places = lax.broadcasted_iota(jnp.int32, (SEG, SEG), 1)
    for seg in range(2):
        part = slice(seg * SEG, (seg + 1) * SEG)
        same = doc_col[part, :] == doc_row[:, part]
        bias[seg] = jnp.where((sources <= places) & same, 0.0, NEG)
    count = jnp.zeros((SEG, SEG), F32)
    for c in range(K):
        count = count + jnp.where(sources == slots[c : c + 1, :], 1.0, 0.0)
    kept = (doc_col[0:SEG, :] == doc_row[:, SEG : 2 * SEG]) & (count > 0.0)
    bias[2] = jnp.where(kept, jnp.log(jnp.maximum(count, 1.0)), NEG)


def rows_from_ext(ext):
    pick = lax.broadcasted_iota(jnp.int32, (PIECES, D), 1) == ROWS * lax.broadcasted_iota(
        jnp.int32, (PIECES, D), 0
    )
    gains = mm(pick.astype(BF), ext).astype(BF)
    source = lax.broadcasted_iota(jnp.int32, (128, D), 0) - GCOL
    column = lax.broadcasted_iota(jnp.int32, (128, D), 1)
    spread = mm(gains, (source == (column & (GLEN - 1))).astype(BF))
    piece = lax.broadcasted_iota(jnp.int32, (PIECES, D), 0)
    block = lax.broadcasted_iota(jnp.int32, (PIECES, D), 1) // GLEN
    one = jnp.sum(jnp.where(block == piece, spread, 0.0), axis=0, keepdims=True)
    two = jnp.sum(jnp.where(block + D // GLEN == piece, spread, 0.0), axis=0, keepdims=True)
    return one, two


def ext_from_gains(column, gain, two):
    row_id = lax.broadcasted_iota(jnp.int32, (D, 128), 0)
    lane = lax.broadcasted_iota(jnp.int32, (D, 128), 1) - GCOL
    target = (lane == (row_id & (GLEN - 1))).astype(BF)
    piece = lax.broadcasted_iota(jnp.int32, (PIECES, D), 0)
    block = lax.broadcasted_iota(jnp.int32, (PIECES, D), 1) // GLEN
    gain_rows = jnp.where(block == piece, 1.0 / gain, 0.0)
    one = lax.dot_general(
        gain_rows,
        jnp.where(lane == (row_id & (GLEN - 1)), column, 0.0),
        (((1,), (0,)), ((), ())),
        precision=lax.Precision.HIGHEST,
        preferred_element_type=F32,
    )
    laid = jnp.where(block + D // GLEN == piece, two, 0.0)
    packed = (one + mm(laid.astype(BF), target)).astype(BF)
    pick = lax.broadcasted_iota(jnp.int32, (D, PIECES), 0) == ROWS * lax.broadcasted_iota(
        jnp.int32, (D, PIECES), 1
    )
    return mm(pick.astype(BF), packed)


def start_pieces(parts, owner, make):
    base = 0
    for part in parts:
        for i in range(part.shape[0]):
            make(part.at[i], owner(base + i)).start()
        base += part.shape[0]


def head_half(rows, upper_half):
    blank = jnp.zeros_like(rows)
    return jnp.concatenate([blank, rows] if upper_half else [rows, blank], axis=0)


PROB_ROWS = 2 * 768 + 1024


def params(mib):
    return pltpu.CompilerParams(vmem_limit_bytes=mib * 1024 * 1024)


def shape(*dims, dtype=BF):
    return jax.ShapeDtypeStruct(dims, dtype)


def block_rows(d, size):
    return pl.ds(pl.multiple_of(d * size, size), size)


SPOTS = [(seg, ib) for seg in range(3) for ib in range(2)]


def spot(seg, ib):
    key_first = SEG if seg == 1 else 0
    key_count = SEG if seg == 2 else 256 * (ib + 1)
    column = (0 if seg == 0 else SEG) + 256 * ib
    base = 768 * seg + ib * (SEG if seg == 2 else 256)
    return key_first, key_count, column, base


def attention_kernel(owner, count, *refs):
    x_hbm, bias_hbm = refs[:2]
    parts = refs[2 : 2 + count]
    (
        w_o,
        vtok_o,
        qkvt_o,
        hidt_o,
        gatet,
        gains,
        probs,
        local_t,
        mem_t,
        inv_sums,
        mixed_t,
        x,
        bias,
        w,
        ktok,
        vtok,
        qkvt,
        hidt,
        in_sem,
        out_sem,
    ) = refs[2 + count :]
    pair = pl.program_id(0)
    late_out = [(w, w_o), (vtok, vtok_o), (qkvt, qkvt_o), (hidt, hidt_o)]

    @pl.when(pair == 0)
    def _():
        start_pieces(
            parts,
            owner,
            lambda src, d: pltpu.make_async_copy(src, w.at[block_rows(d, ROWS)], in_sem.at[0]),
        )
        pltpu.make_async_copy(x_hbm, x, in_sem.at[1]).start()
        pltpu.make_async_copy(bias_hbm, bias, in_sem.at[2]).start()
        pltpu.make_async_copy(w_o, w, in_sem.at[0]).wait()
        pltpu.make_async_copy(x_hbm, x, in_sem.at[1]).wait()
        g_one, g_two = rows_from_ext(w[:, 3 * D :])
        gains[...] = jnp.concatenate([g_one, g_two], axis=0)
        for block in range(4):
            rows = slice(256 * block, 256 * block + 256)
            xf = x[rows, :].astype(F32)
            factor = lax.rsqrt(jnp.mean(xf * xf, axis=1, keepdims=True) + 1e-06)
            hid = (xf * factor * g_one).astype(BF)
            hidt[:, rows] = hid.T
            query = mm(hid, w[:, 0:D]).astype(BF) * 0.125
            qkvt[0:D, rows] = query.T
            key = mm(hid, w[:, D : 2 * D]).astype(BF)
            ktok[rows, :] = key
            value = mm(hid, w[:, 2 * D : 3 * D]).astype(BF)
            vtok[rows, :] = value
            qkvt[D : 2 * D, rows] = key.T
            qkvt[2 * D : 3 * D, rows] = value.T
            gatet[:, rows] = jax.nn.sigmoid(mm(hid, w[:, 3 * D :])).T[0:H, :]
        for i, (src, dst) in enumerate(late_out):
            pltpu.make_async_copy(src, dst, out_sem.at[i]).start()
        pltpu.make_async_copy(bias_hbm, bias, in_sem.at[2]).wait()

    lanes = block_rows(pair, 128)
    gates = [gatet[pl.ds(2 * pair + hh, 1), :] for hh in range(2)]

    def head_rows(third, hh, first, count):
        start = pl.multiple_of(third * D + pair * 128 + hh * HD, HD)
        return qkvt[pl.ds(start, HD), first : first + count]

    def scores(hh, seg, ib):
        key_first, key_count, column, base = spot(seg, ib)
        query = head_half(head_rows(0, hh, column, 256), hh)
        return mm(ktok[key_first : key_first + key_count, lanes], query)

    def soft(score, hh, seg, ib):
        key_first, key_count, column, base = spot(seg, ib)
        score = score + bias[seg, 0:key_count, 256 * ib : 256 * ib + 256]
        peak = jnp.max(score, axis=0, keepdims=True)
        if seg == 2:
            peak = jnp.maximum(peak, 0.0)
        expo = jnp.exp(score - peak)
        total = jnp.sum(expo, axis=0, keepdims=True)
        if seg == 2:
            total = total + jnp.exp(-peak)
        expo_b = expo.astype(BF)
        probs[0, hh, base : base + key_count, :] = expo_b
        return expo_b, 1.0 / total

    held = {}

    def close(expo_b, inverse, hh, seg, ib):
        key_first, key_count, column, base = spot(seg, ib)
        rows = slice(hh * HD, (hh + 1) * HD)
        found = mm(head_rows(2, hh, key_first, key_count), expo_b) * inverse
        here = gates[hh][:, column : column + 256]
        if seg < 2:
            local_t[rows, column : column + 256] = found.astype(BF)
            inv_sums[0, hh : hh + 1, column : column + 256] = inverse
            if seg == 0:
                mixed_t[rows, column : column + 256] = (here * found).astype(BF)
            else:
                held[hh, ib] = here * found
            return
        mem_t[rows, 256 * ib : 256 * ib + 256] = found.astype(BF)
        inv_sums[0, 2 + hh : 3 + hh, 256 * ib : 256 * ib + 256] = inverse
        mixed_t[rows, column : column + 256] = (
            held.pop((hh, ib)) + (1.0 - here) * found
        ).astype(BF)

    order = [(hh, seg, ib) for ib in range(2) for seg in range(3) for hh in range(2)]
    waiting = scores(*order[0])
    late = None
    for i, item in enumerate(order):
        score = waiting
        if i + 1 < len(order):
            waiting = scores(*order[i + 1])
        expo_b, inverse = soft(score, *item)
        if late is not None:
            close(*late)
        late = (expo_b, inverse) + item
    close(*late)
    inv_sums[0, 2:4, SEG:] = jnp.zeros((2, SEG), F32)

    @pl.when(pair == 3)
    def _():
        for i, (src, dst) in enumerate(late_out):
            pltpu.make_async_copy(src, dst, out_sem.at[i]).wait()


def attention(x, bias, parts, owner, deps=()):
    count_in = 2 + len(parts)

    def body(*refs):
        attention_kernel(owner, len(parts), *refs[:count_in], *refs[count_in + len(deps) :])

    const2 = lambda p: (0, 0)
    down = lambda p: (p, 0)
    return pl.pallas_call(
        body,
        grid=(4,),
        in_specs=[ANY] * (count_in + len(deps)),
        out_specs=[
            ANY,
            ANY,
            ANY,
            ANY,
            pl.BlockSpec((H, SEQ), const2),
            pl.BlockSpec((2, D), const2),
            pl.BlockSpec((1, 2, PROB_ROWS, 256), lambda p: (p, 0, 0, 0)),
            pl.BlockSpec((128, SEQ), down),
            pl.BlockSpec((128, SEG), down),
            pl.BlockSpec((1, 4, SEQ), lambda p: (p, 0, 0)),
            pl.BlockSpec((128, SEQ), down),
        ],
        out_shape=[
            shape(D, EXT),
            shape(SEQ, D),
            shape(3 * D, SEQ),
            shape(D, SEQ),
            shape(H, SEQ, dtype=F32),
            shape(2, D, dtype=F32),
            shape(4, 2, PROB_ROWS, 256),
            shape(D, SEQ),
            shape(D, SEG),
            shape(4, 4, SEQ, dtype=F32),
            shape(D, SEQ),
        ],
        scratch_shapes=[
            pltpu.VMEM((SEQ, D), BF),
            pltpu.VMEM((3, SEG, SEG), F32),
            pltpu.VMEM((D, EXT), BF),
            pltpu.VMEM((SEQ, D), BF),
            pltpu.VMEM((SEQ, D), BF),
            pltpu.VMEM((3 * D, SEQ), BF),
            pltpu.VMEM((D, SEQ), BF),
            pltpu.SemaphoreType.DMA((3,)),
            pltpu.SemaphoreType.DMA((4,)),
        ],
        compiler_params=params(60),
        cost_estimate=pl.CostEstimate(
            flops=18_000_000_000, bytes_accessed=40_000_000, transcendentals=6_000_000
        ),
        name="attention",
    )(x, bias, *parts, *deps)


TILE = 256
TILES = FF // TILE


def ffn_kernel(owner_u, owner_d, count, count_o, *refs):
    x_hbm, cot_hbm, mixt_hbm, gains = refs[:4]
    parts_u = refs[4 : 4 + count]
    parts_d = refs[4 + count : 4 + 2 * count]
    refs = refs[4 + 2 * count :]
    layer_o, d_resid_o, dmix_o, dgain = refs[:4]
    grads_u = refs[4 : 4 + count_o]
    grads_d = refs[4 + count_o : 4 + 2 * count_o]
    (
        x,
        cot,
        mixt,
        w_out,
        w_up,
        w_dn,
        hid,
        hidt,
        resid,
        oacc,
        dacc,
        dmix,
        g_out,
        g_up,
        g_dn,
        held_up,
        held_act,
        acts,
        d_ups,
        factors,
        in_sem,
        out_sem,
    ) = refs[4 + 2 * count_o :]
    per = PIECES // count_o

    def lanes_of(tile):
        return pl.ds(pl.multiple_of((tile % 2) * TILE, TILE), TILE)

    def up_tile(tile):
        return w_up[tile // 2, :, lanes_of(tile)]

    def dn_tile(tile):
        return w_dn[pl.ds(tile * (TILE // ROWS), TILE // ROWS)].reshape(TILE, D)

    def head_up(tile, slot):
        held_up[slot] = mm(hid[...], up_tile(tile))

    def head_act(tile, slot):
        held_act[slot] = mm_nt(cot[...], dn_tile(tile))

    def head(tile, slot):
        head_up(tile, slot)
        head_act(tile, slot)

    def gelu(slot, first, last):
        c0 = 0.7978845608028654
        c1 = 0.044715
        for block in range(first, last):
            rows = slice(64 * block, 64 * block + 64)
            upper = held_up[slot, rows, :]
            square = upper * upper
            tanh = jnp.tanh(upper * (c0 + (c0 * c1) * square))
            half_t = 0.5 * tanh + 0.5
            slope = half_t + upper * (1.0 - tanh * tanh) * (0.5 * c0 + (1.5 * c0 * c1) * square)
            acts[slot, rows, :] = (upper * half_t).astype(BF)
            d_ups[slot, rows, :] = (held_act[slot, rows, :] * slope).astype(BF)

    def tail_out(tile, slot):
        oacc[...] += mm(acts[slot], dn_tile(tile))

    def tail_hid(tile, slot):
        dacc[...] += mm_nt(d_ups[slot], up_tile(tile))

    def tail_dn(tile, slot):
        g_dn[pl.ds(tile * (TILE // ROWS), TILE // ROWS)] = (
            mm_tn(acts[slot], cot[...]).astype(BF).reshape(TILE // ROWS, ROWS, D)
        )

    def tail_up(tile, slot):
        g_up[tile // 2, :, lanes_of(tile)] = mm(hidt[...], d_ups[slot]).astype(BF)

    def tail(tile, slot):
        tail_out(tile, slot)
        tail_hid(tile, slot)
        tail_dn(tile, slot)
        tail_up(tile, slot)

    def spread(step, now):
        later = jnp.minimum(step + 1, TILES - 1)
        before = jnp.maximum(step - 1, 0)
        jobs = (tail_dn, tail_out, head_up, tail_up, tail_hid, head_act)
        count = 16
        for i, job in enumerate(jobs):
            gelu(now, count * i // 6, count * (i + 1) // 6)
            job(later if job in (head_up, head_act) else before, 1 - now)

    start_pieces(
        parts_u,
        owner_u,
        lambda src, d: pltpu.make_async_copy(
            src.at[0], w_out.at[block_rows(d, ROWS), :], in_sem.at[0]
        ),
    )
    pltpu.make_async_copy(mixt_hbm, mixt, in_sem.at[4]).start()
    pltpu.make_async_copy(x_hbm, x, in_sem.at[5]).start()
    start_pieces(
        parts_u,
        owner_u,
        lambda src, d: pltpu.make_async_copy(
            src.at[pl.ds(1, 4)], w_up.at[:, block_rows(d, ROWS), :], in_sem.at[1]
        ),
    )
    start_pieces(
        parts_d,
        owner_d,
        lambda src, d: pltpu.make_async_copy(src, w_dn.at[pl.ds(d * 4, 4)], in_sem.at[2]),
    )
    pltpu.make_async_copy(cot_hbm, cot, in_sem.at[3]).start()
    pltpu.make_async_copy(g_out, w_out, in_sem.at[0]).wait()
    pltpu.make_async_copy(mixt_hbm, mixt, in_sem.at[4]).wait()
    pltpu.make_async_copy(x_hbm, x, in_sem.at[5]).wait()
    dacc[...] = jnp.zeros_like(dacc)
    acts[1] = jnp.zeros((SEQ, TILE), BF)
    d_ups[1] = jnp.zeros((SEQ, TILE), BF)
    for block in range(4):
        rows = slice(256 * block, 256 * block + 256)
        value = x[rows, :].astype(F32) + mm_tn(mixt[:, rows], w_out[...])
        factor = lax.rsqrt(jnp.mean(value * value, axis=1, keepdims=True) + 1e-06)
        normed = (value * factor * gains[1:2, :]).astype(BF)
        factors[rows, :] = factor
        resid[rows, :] = value
        oacc[rows, :] = value
        hid[rows, :] = normed
        hidt[:, rows] = normed.T
    pltpu.make_async_copy(g_up, w_up, in_sem.at[1]).wait()
    pltpu.make_async_copy(g_dn, w_dn, in_sem.at[2]).wait()
    pltpu.make_async_copy(cot_hbm, cot, in_sem.at[3]).wait()
    head(0, 0)

    @pl.loop(0, TILES)
    def _(step):
        spread(step, step % 2)

    tail(TILES - 1, (TILES - 1) % 2)
    for piece in range(PIECES):
        pltpu.make_async_copy(
            g_up.at[:, block_rows(owner_u(piece), ROWS), :],
            grads_u[piece // per].at[piece % per, pl.ds(1, 4)],
            out_sem.at[0],
        ).start()
        pltpu.make_async_copy(
            g_dn.at[pl.ds(owner_d(piece) * 4, 4)],
            grads_d[piece // per].at[piece % per],
            out_sem.at[1],
        ).start()
    g_two = gains[1:2, :]
    total = jnp.zeros((1, D), F32)
    for block in range(16):
        rows = slice(64 * block, 64 * block + 64)
        value = resid[rows, :]
        factor = factors[rows, :]
        d_hid = dacc[rows, :]
        product = d_hid * value
        total = total + jnp.sum(product * factor, axis=0, keepdims=True)
        inner = jnp.mean(product * g_two, axis=1, keepdims=True)
        d_resid = cot[rows, :].astype(F32) + (
            factor * (d_hid * g_two) - value * (factor * factor * factor * inner)
        )
        x[rows, :] = oacc[rows, :].astype(BF)
        resid[rows, :] = d_resid
        hid[rows, :] = d_resid.astype(BF)
    dgain[...] = total
    pltpu.make_async_copy(x, layer_o, out_sem.at[2]).start()
    pltpu.make_async_copy(resid, d_resid_o, out_sem.at[3]).start()
    g_out[...] = mm(mixt[...], hid[...]).astype(BF)
    for piece in range(PIECES):
        pltpu.make_async_copy(
            g_out.at[block_rows(owner_u(piece), ROWS), :],
            grads_u[piece // per].at[piece % per, 0],
            out_sem.at[5],
        ).start()
    dmix[...] = mm_nt(w_out[...], hid[...]).astype(BF)
    pltpu.make_async_copy(dmix, dmix_o, out_sem.at[4]).start()
    pltpu.make_async_copy(g_up, w_up, out_sem.at[0]).wait()
    pltpu.make_async_copy(g_dn, w_dn, out_sem.at[1]).wait()
    pltpu.make_async_copy(x, layer_o, out_sem.at[2]).wait()
    pltpu.make_async_copy(resid, d_resid_o, out_sem.at[3]).wait()
    pltpu.make_async_copy(g_out, w_out, out_sem.at[5]).wait()
    pltpu.make_async_copy(dmix, dmix_o, out_sem.at[4]).wait()


def ffn(x, cot, mixed_t, gains, parts_u, parts_d, owner_u, owner_d, count_o):
    def body(*refs):
        ffn_kernel(owner_u, owner_d, len(parts_u), count_o, *refs)

    return pl.pallas_call(
        body,
        in_specs=[ANY, ANY, ANY, pl.BlockSpec(memory_space=pltpu.VMEM)]
        + [ANY] * (len(parts_u) + len(parts_d)),
        out_specs=[ANY, ANY, ANY, pl.BlockSpec(memory_space=pltpu.VMEM)] + [ANY] * (2 * count_o),
        out_shape=[
            shape(SEQ, D),
            shape(SEQ, D, dtype=F32),
            shape(D, SEQ),
            shape(1, D, dtype=F32),
        ]
        + [shape(PIECES // count_o, 5, ROWS, D)] * count_o
        + [shape(PIECES // count_o, 4, ROWS, D)] * count_o,
        scratch_shapes=[
            pltpu.VMEM((SEQ, D), BF),
            pltpu.VMEM((SEQ, D), BF),
            pltpu.VMEM((D, SEQ), BF),
            pltpu.VMEM((D, D), BF),
            pltpu.VMEM((4, D, D), BF),
            pltpu.VMEM((FF // ROWS, ROWS, D), BF),
            pltpu.VMEM((SEQ, D), BF),
            pltpu.VMEM((D, SEQ), BF),
            pltpu.VMEM((SEQ, D), F32),
            pltpu.VMEM((SEQ, D), F32),
            pltpu.VMEM((SEQ, D), F32),
            pltpu.VMEM((D, SEQ), BF),
            pltpu.VMEM((D, D), BF),
            pltpu.VMEM((4, D, D), BF),
            pltpu.VMEM((FF // ROWS, ROWS, D), BF),
            pltpu.VMEM((2, SEQ, TILE), F32),
            pltpu.VMEM((2, SEQ, TILE), F32),
            pltpu.VMEM((2, SEQ, TILE), BF),
            pltpu.VMEM((2, SEQ, TILE), BF),
            pltpu.VMEM((SEQ, 1), F32),
            pltpu.SemaphoreType.DMA((6,)),
            pltpu.SemaphoreType.DMA((6,)),
        ],
        compiler_params=params(60),
        cost_estimate=pl.CostEstimate(
            flops=25_000_000_000, bytes_accessed=25_000_000, transcendentals=2_000_000
        ),
        name="feed_forward",
    )(x, cot, mixed_t, gains, *parts_u, *parts_d)


def attention_back_kernel(first, pairs, spans, owner, count_o, *refs):
    (gatet, w_hbm, hidt_hbm, probs, local_t, mem_t, inv_sums, dmix_t, qt, kt, vtok) = refs[:11]
    refs = refs[11:]
    last = len(spans) > 0
    if last:
        gains, dgain_two = refs[:2]
        befores = [refs[2 + 3 * i : 5 + 3 * i] for i in range(len(spans))]
        refs = refs[2 + 3 * len(spans) :]
    else:
        count_o = 1
    dqkvt, d_gates, *refs = refs
    if not last:
        weighted = refs[0]
        refs = refs[1:]
    grads = refs[:count_o]
    w, hidt, scratch, gate_rows, g_ext, d_probs, d_scores, in_sem, out_sem = refs[count_o:]
    pair = pl.program_id(0)
    per = PIECES // count_o

    def before_columns():
        return [
            pltpu.make_async_copy(
                before[2].at[third],
                g_ext.at[:, pl.ds(third * D + at * 128, count * 128)],
                in_sem.at[2],
            )
            for third in range(3)
            for (at, count), before in zip(spans, befores)
        ]

    @pl.when(pair == 0)
    def _():
        pltpu.make_async_copy(hidt_hbm, hidt, in_sem.at[0]).start()
        pltpu.make_async_copy(w_hbm, w, in_sem.at[1]).start()
        if last:
            for copy in before_columns():
                copy.start()

    ups = {}
    dots = {}
    for hh in range(2):
        rows = slice(hh * HD, (hh + 1) * HD)
        gate = gatet[pl.ds(2 * (first + pair) + hh, 1), :]
        d_mix = dmix_t[rows, :].astype(F32)
        local = local_t[rows, :].astype(F32)
        mem = mem_t[rows, :].astype(F32)
        inv_local = inv_sums[0, hh : hh + 1, :]
        inv_mem = inv_sums[0, 2 + hh : 3 + hh, 0:SEG]
        d_local = (d_mix * (gate * inv_local)).astype(BF)
        d_mem = (d_mix[:, SEG:] * ((1.0 - gate[:, SEG:]) * inv_mem)).astype(BF)
        dot_local = jnp.sum(d_local.astype(F32) * local, axis=0, keepdims=True)
        dot_mem = jnp.sum(d_mem.astype(F32) * mem, axis=0, keepdims=True)
        plain_local = jnp.sum(d_mix * local, axis=0, keepdims=True)
        plain_mem = jnp.sum(d_mix[:, SEG:] * mem, axis=0, keepdims=True)
        d_gate = gate * (1.0 - gate) * (
            plain_local - jnp.concatenate([jnp.zeros((1, SEG), F32), plain_mem], axis=1)
        )
        d_gates[0, hh : hh + 1, :] = d_gate
        gate_rows[pl.ds(2 * pair + hh, 1), :] = d_gate
        for seg, ib in SPOTS:
            column = spot(seg, ib)[2]
            if seg == 2:
                ups[hh, seg, ib] = d_mem[:, 256 * ib : 256 * ib + 256]
                dots[hh, seg, ib] = dot_mem[:, 256 * ib : 256 * ib + 256]
            else:
                ups[hh, seg, ib] = d_local[:, column : column + 256]
                dots[hh, seg, ib] = dot_local[:, column : column + 256]

    sums_of = {}

    def add(key, value):
        sums_of[key] = value if key not in sums_of else sums_of[key] + value

    def begin(slot, hh, seg, ib):
        key_first, key_count, column, base = spot(seg, ib)
        d_probs[slot, 0:key_count, :] = mm(
            vtok[key_first : key_first + key_count, :], head_half(ups[hh, seg, ib], hh)
        )

    def middle(slot, part, hh, seg, ib):
        key_first, key_count, column, base = spot(seg, ib)
        size = key_count // 4
        for step in range(size // 64):
            at = part * size + 64 * step
            expo = probs[0, hh, base + at : base + at + 64, :].astype(F32)
            d_scores[slot, at : at + 64, :] = (
                expo * (d_probs[slot, at : at + 64, :] - dots[hh, seg, ib])
            ).astype(BF)

    def close(slot, part, hh, seg, ib):
        key_first, key_count, column, base = spot(seg, ib)
        rows = slice(hh * HD, (hh + 1) * HD)
        if part == 0:
            value = mm(kt[rows, key_first : key_first + key_count], d_scores[slot, 0:key_count, :])
            add((0, hh, column // 256), value)
            return
        if part == 1:
            value = mm_nt(qt[rows, column : column + 256], d_scores[slot, 0:key_count, :])
        else:
            value = mm_nt(ups[hh, seg, ib], probs[0, hh, base : base + key_count, :])
        for block in range(key_count // 256):
            place = key_first // 256 + block
            add((part, hh, place), value[:, 256 * block : 256 * block + 256])

    order = [(hh, seg, ib) for seg in (0, 2, 1) for ib in range(2) for hh in range(2)]
    begin(0, *order[0])
    for i in range(len(order) + 1):
        if i < len(order):
            middle(i % 2, 0, *order[i])
        if i > 0:
            close((i - 1) % 2, 2, *order[i - 1])
        if i < len(order):
            middle(i % 2, 1, *order[i])
        if i > 0:
            close((i - 1) % 2, 0, *order[i - 1])
        if i < len(order):
            middle(i % 2, 2, *order[i])
        if i > 0:
            close((i - 1) % 2, 1, *order[i - 1])
        if i < len(order):
            middle(i % 2, 3, *order[i])
        if i + 1 < len(order):
            begin((i + 1) % 2, *order[i + 1])
    for (third, hh, place), value in sums_of.items():
        if third == 0:
            value = value * 0.125
        rows = slice(hh * HD, (hh + 1) * HD)
        dqkvt[third, rows, 256 * place : 256 * place + 256] = value.astype(BF)
    scratch[:, block_rows(pair, 128), :] = dqkvt[...]

    @pl.when(pair == pairs - 1)
    def _():
        pltpu.make_async_copy(hidt_hbm, hidt, in_sem.at[0]).wait()
        pltpu.make_async_copy(w_hbm, w, in_sem.at[1]).wait()
        sums = jnp.zeros((D, 128), F32)
        for third in range(3):
            grad = mm_nt(hidt[...], scratch[third])
            start = third * D + first * 128
            for part in range(pairs):
                columns = slice(start + 128 * part, start + 128 * part + 128)
                sums = sums + grad[:, 128 * part : 128 * part + 128] * w[:, columns].astype(F32)
            if last:
                g_ext[:, start : start + 128 * pairs] = grad.astype(BF)
            else:
                g_ext[third] = grad.astype(BF)
        if last:
            d_gate_b = jnp.concatenate(
                [before[1][i] for before in befores for i in range(before[1].shape[0])]
                + [gate_rows[0 : 2 * pairs, :], jnp.zeros((120, SEQ), F32)],
                axis=0,
            ).astype(BF)
            grad = mm_nt(hidt[...], d_gate_b)
            gate_lane = lax.broadcasted_iota(jnp.int32, (D, 128), 1) < H
            sums = sums + jnp.where(gate_lane, grad * w[:, 3 * D :].astype(F32), 0.0)
            for before in befores:
                sums = sums + before[0][...]
            column = jnp.sum(sums, axis=1, keepdims=True)
            g_ext[:, 3 * D :] = (grad + ext_from_gains(column, gains[0:1, :], dgain_two[...])).astype(
                BF
            )
        if not last:
            weighted[...] = sums
            pltpu.make_async_copy(g_ext, grads[0], out_sem).start()
            pltpu.make_async_copy(g_ext, grads[0], out_sem).wait()
        else:
            for copy in before_columns():
                copy.wait()
            for piece in range(PIECES):
                pltpu.make_async_copy(
                    g_ext.at[block_rows(owner(piece), ROWS), :],
                    grads[piece // per].at[piece % per],
                    out_sem,
                ).start()
            pltpu.make_async_copy(w, g_ext, out_sem).wait()


def attention_back(
    first, pairs, gatet, w, hidt, saved, dmix_t, qkvt, vtok, owner, count_o, extra=(), befores=(), deps=()
):
    last = len(extra) > 0
    spans = [span for span, *_ in befores]
    extra = (*extra, *(array for _, *arrays in befores for array in arrays))
    const2 = lambda p: (0, 0)
    count_in = 11 + len(extra)

    def body(*refs):
        attention_back_kernel(
            first, pairs, spans, owner, count_o, *refs[:count_in], *refs[count_in + len(deps) :]
        )

    extra_specs = []
    if last:
        extra_specs = [
            pl.BlockSpec((2, D), const2),
            pl.BlockSpec((1, D), const2),
        ]
        for _, count in spans:
            extra_specs += [
                pl.BlockSpec((D, 128), const2),
                pl.BlockSpec((count, 2, SEQ), lambda p: (0, 0, 0)),
                ANY,
            ]
    sums_spec = [] if last else [pl.BlockSpec((D, 128), const2)]
    sums_shape = [] if last else [shape(D, 128, dtype=F32)]
    return pl.pallas_call(
        body,
        grid=(pairs,),
        in_specs=[
            pl.BlockSpec((H, SEQ), const2),
            ANY,
            ANY,
            pl.BlockSpec((1, 2, PROB_ROWS, 256), lambda p: (first + p, 0, 0, 0)),
            pl.BlockSpec((128, SEQ), lambda p: (first + p, 0)),
            pl.BlockSpec((128, SEG), lambda p: (first + p, 0)),
            pl.BlockSpec((1, 4, SEQ), lambda p: (first + p, 0, 0)),
            pl.BlockSpec((128, SEQ), lambda p: (first + p, 0)),
            pl.BlockSpec((128, SEQ), lambda p: (first + p, 0)),
            pl.BlockSpec((128, SEQ), lambda p: (4 + first + p, 0)),
            pl.BlockSpec((SEQ, 128), lambda p: (0, first + p)),
        ]
        + extra_specs
        + [ANY] * len(deps),
        out_specs=[
            pl.BlockSpec((3, 128, SEQ), lambda p: (0, p, 0)),
            pl.BlockSpec((1, 2, SEQ), lambda p: (p, 0, 0)),
        ]
        + sums_spec
        + [ANY] * (count_o if last else 1),
        out_shape=[shape(3, 128 * pairs, SEQ), shape(pairs, 2, SEQ, dtype=F32)]
        + sums_shape
        + ([shape(PIECES // count_o, ROWS, EXT)] * count_o if last else [shape(3, D, 128 * pairs)]),
        scratch_shapes=[
            pltpu.VMEM((D, EXT), BF),
            pltpu.VMEM((D, SEQ), BF),
            pltpu.VMEM((3, 128 * pairs, SEQ), BF),
            pltpu.VMEM((8, SEQ), F32),
            pltpu.VMEM((D, EXT) if last else (3, D, 128 * pairs), BF),
            pltpu.VMEM((2, SEG, 256), F32),
            pltpu.VMEM((2, SEG, 256), BF),
            pltpu.SemaphoreType.DMA((3,)),
            pltpu.SemaphoreType.DMA,
        ],
        compiler_params=params((60, 24, 0, 24)[first]),
        cost_estimate=pl.CostEstimate(
            flops=11_000_000_000, bytes_accessed=20_000_000, transcendentals=0
        ),
        name="attention_back",
    )(gatet, w, hidt, *saved, dmix_t, qkvt, qkvt, vtok, *extra, *deps)


def input_back_kernel(x, d_resid, gains, w, parts, gates, grad_in):
    d_gate = jnp.concatenate(
        [gate[i] for gate in gates for i in range(gate.shape[0])] + [jnp.zeros((120, 256), F32)],
        axis=0,
    ).astype(BF)
    d_hid = mm(w[:, 3 * D :], d_gate)
    for third in range(3):
        rows = jnp.concatenate([part[third] for part in parts], axis=0)
        d_hid = d_hid + mm(w[:, third * D : third * D + D], rows)
    d_hid = d_hid.T
    xf = x[...].astype(F32)
    factor = lax.rsqrt(jnp.mean(xf * xf, axis=1, keepdims=True) + 1e-06)
    scaled = d_hid * gains[0:1, :]
    inner = jnp.mean(scaled * xf, axis=1, keepdims=True)
    grad_in[...] = (
        d_resid[...] + factor * scaled - xf * (factor * factor * factor * inner)
    ).astype(BF)


def input_back(x, d_resid, gains, w, parts, gates, deps=()):
    count = len(parts)

    def body(*refs):
        input_back_kernel(*refs[:4], refs[4 : 4 + count], refs[4 + count : 4 + 2 * count], refs[-1])

    const2 = lambda i: (0, 0)
    rows = lambda i: (i, 0)
    across = lambda i: (0, 0, i)
    return pl.pallas_call(
        body,
        grid=(4,),
        in_specs=[
            pl.BlockSpec((256, D), rows),
            pl.BlockSpec((256, D), rows),
            pl.BlockSpec((2, D), const2),
            pl.BlockSpec((D, EXT), const2),
        ]
        + [pl.BlockSpec((3, part.shape[1], 256), across) for part in parts]
        + [pl.BlockSpec((gate.shape[0], 2, 256), across) for gate in gates]
        + [ANY] * len(deps),
        out_specs=pl.BlockSpec((256, D), rows),
        out_shape=shape(SEQ, D),
        compiler_params=params(20),
        cost_estimate=pl.CostEstimate(
            flops=5_000_000_000, bytes_accessed=9_000_000, transcendentals=0
        ),
        name="input_back",
    )(x, d_resid, gains, w, *parts, *gates, *deps)


def ext_rows(qkv, gate, gains):
    count = qkv.shape[0]
    blank = jnp.zeros((count, 128 - GCOL - gains.shape[1]), BF)
    return jnp.concatenate([qkv, gate, gains, blank], axis=1)


def local(
    n, inputs, cotangent, doc_ids, slot_ids, qkv_flat, out_flat, norm_gains, gate_flat, up_flat, down_flat
):
    split = n == PIECES
    count_o = 2 if split else 1
    owner_x = owner_fn(split, True)
    owner_y = owner_fn(split, False)
    doc_row = doc_ids.reshape(1, SEQ)
    doc_col = doc_ids.reshape(SEQ, 1)
    slots = slot_ids.reshape(SEG, K).T
    bias = pl.pallas_call(
        bias_kernel,
        out_shape=shape(3, SEG, SEG, dtype=F32),
        name="masks",
    )(doc_row, doc_col, slots)
    if split:
        gains_rows = jnp.broadcast_to(norm_gains.reshape(1, GLEN), (ROWS, GLEN))
        shard_a = ext_rows(qkv_flat.reshape(ROWS, 3 * D), gate_flat.reshape(ROWS, H), gains_rows)
        shard_f = jnp.concatenate(
            [
                out_flat.reshape(1, ROWS, D),
                up_flat.reshape(ROWS, 4, D).transpose(1, 0, 2),
                down_flat.reshape(4, ROWS, D),
            ]
        )
        shard_a, shard_f = lax.optimization_barrier((shard_a, shard_f))
        z_a = gather_z(shard_a)
        plane_a = after(gather_plane(z_a), bias)
        parts_a = gather_core(plane_a)
        z_f = gather_z(shard_f)
        z_u, z_d = z_f[:, :5], z_f[:, 5:]
        wide_u = jnp.concatenate([z_u, perm_bit(z_u, 1)])
        wide_d = jnp.concatenate([z_d, perm_bit(z_d, 2)])
        halves_u = [wide_u, perm_bit(wide_u, 2)]
        halves_d = [wide_d, perm_bit(wide_d, 1)]
        deps = (wide_u, wide_d)
    else:
        whole = [
            lax.all_gather(v, AXES, axis=0, tiled=True)
            for v in (qkv_flat, out_flat, norm_gains, gate_flat, up_flat, down_flat)
        ]
        gains_rows = jnp.repeat(whole[2].reshape(PIECES, GLEN), ROWS, axis=0)
        ext = ext_rows(whole[0].reshape(D, 3 * D), whole[3].reshape(D, H), gains_rows)
        parts_a = (ext.reshape(PIECES, ROWS, EXT),)
        parts_u = (
            jnp.concatenate(
                [
                    whole[1].reshape(PIECES, 1, ROWS, D),
                    whole[4].reshape(PIECES, ROWS, 4, D).transpose(0, 2, 1, 3),
                ],
                axis=1,
            ),
        )
        parts_d = (whole[5].reshape(PIECES, 4, ROWS, D),)
        deps = ()
    w_ext, vtok, qkvt, hidt, gatet, gains, *saved, mixed_t = attention(
        inputs, bias, parts_a, owner_x, deps
    )
    if split:
        far_u, far_d = after((halves_u[1], halves_d[1]), gatet)
        parts_u = gather_core((wide_u, far_u))
        parts_d = gather_core((wide_d, far_d))
    layer_out, d_resid, dmix_t, dgain_two, *grads_f = ffn(
        inputs, cotangent, mixed_t, gains, parts_u, parts_d, owner_x, owner_y, count_o
    )
    shared = (gatet, w_ext, hidt, saved, dmix_t, qkvt, vtok, owner_x, count_o)
    d_one, gates_one, *rest_one = attention_back(0, 1, *shared)
    deps = ()
    if split:
        keep_u, send_u, keep_d, send_d = grads_f
        got_u, got_d = after((perm_core(send_u), perm_core(send_d)), gates_one)
        firsts = (
            add(keep_u[:8], got_u[:8]),
            add(keep_u[8:], got_u[8:]).astype(BF),
            add(keep_d[:8], got_d[:8]),
            add(keep_d[8:], got_d[8:]).astype(BF),
        )
        deps = firsts
    d_two, gates_two, *rest_two = attention_back(1, 2, *shared, deps=deps)
    if split:
        got_u, got_d = after((perm_bit(firsts[1], 2), perm_bit(firsts[3], 1)), gates_two)
        seconds = (
            add(firsts[0][:4], got_u[:4]),
            add(firsts[0][4:], got_u[4:]).astype(BF),
            add(firsts[2][:4], got_d[:4]),
            add(firsts[2][4:], got_d[4:]).astype(BF),
        )
        deps = seconds
    d_three, gates_three, *grads_a = attention_back(
        3,
        1,
        *shared,
        extra=(gains, dgain_two),
        befores=(
            ((0, 1), rest_one[0], gates_one, rest_one[1]),
            ((1, 2), rest_two[0], gates_two, rest_two[1]),
        ),
        deps=deps,
    )
    deps = ()
    if split:
        keep_a, send_a = grads_a
        got_a = perm_core(send_a)
        got_u, got_d = after((perm_bit(seconds[1], 1), perm_bit(seconds[3], 2)), gates_three)
        total_f = jnp.concatenate([add(seconds[0], got_u), add(seconds[2], got_d)], axis=1)
        sends_f = [total_f[k].astype(BF) for k in (1, 2, 3)]
        (got_a,) = after((got_a,), *sends_f)
        sends_a = [
            add(keep_a[4 * k : 4 * k + 4], got_a[4 * k : 4 * k + 4]).astype(BF) for k in (1, 2, 3)
        ]
        deps = sends_a
    grad_input = input_back(
        inputs,
        d_resid,
        gains,
        w_ext,
        (d_one, d_two, d_three),
        (gates_one, gates_two, gates_three),
        deps,
    )
    if split:
        plane = after([perm_bit(sends_a[k - 1], k) for k in (1, 2, 3)], grad_input)
        total_a = add(keep_a[:4], got_a[:4])
        for got in plane:
            total_a = add(total_a, got)
        sends_z = [total_a[k].astype(BF) for k in (1, 2, 3)]
        sum_f = total_f[0]
        for got in after([perm_z(sends_f[k - 1], k) for k in (1, 2, 3)], *sends_z):
            sum_f = add(sum_f, got)
        sum_a = total_a[0]
        for k in (1, 2, 3):
            sum_a = add(sum_a, perm_z(sends_z[k - 1], k))
        grad_out = sum_f[0].reshape(-1)
        grad_up = sum_f[1:5].transpose(1, 0, 2).reshape(-1)
        grad_down = sum_f[5:].reshape(-1)
        grad_qkv = sum_a[:, : 3 * D].reshape(-1)
        grad_gate = sum_a[:, 3 * D : 3 * D + H].reshape(-1)
        grad_gains = sum_a[0, 3 * D + GCOL : 3 * D + GCOL + GLEN]
    else:

        def scatter(v):
            return lax.psum_scatter(
                v.astype(F32).reshape(-1), AXES, scatter_dimension=0, tiled=True
            )

        grad_out = scatter(grads_f[0][:, 0])
        grad_up = scatter(grads_f[0][:, 1:].transpose(0, 2, 1, 3))
        grad_down = scatter(grads_f[1])
        ext = grads_a[0]
        grad_qkv = scatter(ext[:, :, : 3 * D])
        grad_gate = scatter(ext[:, :, 3 * D : 3 * D + H])
        grad_gains = scatter(ext[:, 0, 3 * D + GCOL : 3 * D + GCOL + GLEN])
    return (layer_out, grad_input, grad_qkv, grad_out, grad_gains, grad_gate, grad_up, grad_down)


def solution(mesh):
    n = mesh.shape["dp"] * mesh.shape["fsdp"]

    def per_device(*args):
        return local(n, *args)

    rows = P(AXES, None)
    flat = P(AXES)
    return jax.shard_map(
        per_device,
        mesh=mesh,
        in_specs=(rows, rows, rows, P(AXES, None, None), flat, flat, flat, flat, flat, flat),
        out_specs=(rows, rows, flat, flat, flat, flat, flat, flat),
        check_vma=False,
    )
```
